32 devices in a mesh: blk: 8 (over z, y), rhs: 4 (over x, core).
Axes of the slice: x: 2, y: 2, z: 4, core: 2. Of those that a mesh axis runs over, the one named last changes fastest.
Arguments:
- strips: float32 [64, 25, 128, 128], P('blk'), may hold values from -0.109375 to 0.109375
- near_cols: int32 [64, 25], P('blk'), may hold values from 0 to 63, as said below
- vector_block: float32 [8192, 2048], P(('blk', 'rhs')), may hold values from -6 to 6
- basis: float32 [4, 8192, 2048], P(None, ('blk', 'rhs')), may hold values from -0.0625 to 0.0625
Outputs:
- new_block: float32 [8192, 2048], P(('blk', 'rhs'))
- coeffs: float32 [4, 16, 128, 128], replicated
- factor: float32 [16, 128, 128], replicated
The draws below stay inside these ranges and needn't reach their ends.
Inputs may be any that keep to these rules, and one draw needn't show every extreme that they name: `near_cols`: each row block has 25 distinct column blocks; slot 0 is the row block itself; every column block lies within 24 blocks of its row block, counted cyclically modulo 64, and some row block has a column block exactly 24 blocks above it.
All inputs are finite; a program needn't handle non-finite values.
Results may differ from the reference program's by a relative error of at most 0.0003.
Values sent between devices are 32-bit elements; how exact they have to be, the bound alone decides.
No kernel may reach another device: no remote copies, remote signals or barrier semaphores. Data moves between devices by JAX's collectives and lax.ppermute only.
A program may use at most 256 MiB of HBM per device.

```python
import jax
import jax.numpy as jnp
from jax import lax

BLOCK = 128
NEAR = 25
NRHS = 2048
GROUP = 128
BASIS = 4
RB = 64
ROWS = 8192
BAND = 24


def draw_near_cols(key, part):
    offsets_all = jnp.concatenate([jnp.arange(-BAND, 0), jnp.arange(1, BAND + 1)]).astype(jnp.int32)
    row_keys = jax.random.split(jax.random.fold_in(key, 7), RB)
    perms = jax.vmap(lambda single: jax.random.permutation(single, offsets_all))(row_keys)
    chosen = jax.random.randint(jax.random.fold_in(key, 11), (), 0, RB)
    slots = jnp.arange(2 * BAND)[None, :]
    leading = perms[:, :1]
    forced = jnp.where(perms == BAND, leading, jnp.where(slots == 0, BAND, perms))
    row_ids = jnp.arange(RB)[:, None]
    perms = jnp.where(row_ids == chosen, forced, perms)
    offsets = jnp.concatenate([jnp.zeros((RB, 1), jnp.int32), perms[:, :NEAR - 1]], axis=1)
    return jnp.mod(row_ids + offsets, RB).astype(jnp.int32)


def levels(stream_key, shape, cuts, smallest, top_value):
    def one(axis_at, shards_of):
        heights = jax.random.uniform(jax.random.fold_in(jax.random.fold_in(stream_key, 6), axis_at), (shards_of,), jnp.float32, smallest / len(cuts), top_value / len(cuts))
        return jnp.repeat(jnp.exp(heights), shape[axis_at] // shards_of).reshape((-1,) + (1,) * (len(shape) - axis_at - 1))

    loudness = one(*cuts[0])
    for cut in cuts[1:]:
        loudness = loudness * one(*cut)
    return loudness


def normal_values(rng, shape, scale, limit, cuts=(), kind=jnp.bfloat16):
    entries = scale * jax.random.normal(rng, shape, jnp.float32)
    if cuts:
        entries = entries * levels(rng, shape, cuts, -0.22, 0.18)
    return jnp.clip(entries, -limit, limit).astype(kind)


def setup_inputs(seed: int = 0) -> dict:
    key_list = jax.random.split(jax.random.key(seed), 5)
    strips = normal_values(key_list[0], (RB, NEAR, BLOCK, BLOCK), (NEAR * BLOCK) ** -0.5, 0.109375, ((0, 8),), jnp.float32)
    near_cols = draw_near_cols(jax.random.fold_in(key_list[4], 71), 0)
    vector_block = normal_values(key_list[2], (ROWS, NRHS), 1.0, 6.0, ((0, 32),), jnp.float32)
    basis = normal_values(key_list[3], (BASIS, ROWS, NRHS), ROWS ** -0.5, 0.0625, ((1, 32),), jnp.float32)
    return {"strips": strips, "near_cols": near_cols, "vector_block": vector_block, "basis": basis}


HIGHEST = lax.Precision.HIGHEST

def reference(strips, near_cols, vector_block, basis):
    block = strips.shape[2]
    total_rows, width = vector_block.shape
    pieces = vector_block.reshape(total_rows // block, block, width)

    def one_strip(operands):
        strip, columns = operands
        chosen = pieces[columns.astype(jnp.int32)]
        return jnp.einsum('kab,kbc->ac', strip, chosen, precision=HIGHEST)
    image = lax.map(one_strip, (strips, near_cols)).reshape(total_rows, width)
    groups = width // GROUP
    grouped = image.reshape(total_rows, groups, GROUP)
    basis_grouped = basis.reshape(basis.shape[0], total_rows, groups, GROUP)
    coeffs = jnp.einsum('mnga,ngb->mgab', basis_grouped, grouped, precision=HIGHEST)
    residual = grouped - jnp.einsum('mnga,mgab->ngb', basis_grouped, coeffs, precision=HIGHEST)
    gram = jnp.einsum('nga,ngb->gab', residual, residual, precision=HIGHEST)
    factor = jnp.linalg.cholesky(gram)
    solved = jax.scipy.linalg.solve_triangular(factor, jnp.transpose(residual, (1, 2, 0)), lower=True)
    new_block = jnp.transpose(solved, (2, 0, 1)).reshape(total_rows, width)
    return (new_block, coeffs, factor)
```

```python
import functools

import jax
import jax.numpy as jnp
import numpy as np
from jax import lax
from jax.experimental import pallas as pl
from jax.experimental.pallas import tpu as pltpu
from jax.sharding import PartitionSpec as P

GROUP = 128
BAND = 24
PANEL = 32
CHUNKS = (2, 1, 1)

F32 = jnp.float32
BF16 = jnp.bfloat16
ANY = pl.BlockSpec(memory_space=pl.ANY)
SMEM = pl.BlockSpec(memory_space=pltpu.SMEM)
VMEM = pl.BlockSpec(memory_space=pltpu.VMEM)
LIMIT = 50 * 1024 * 1024


def params(**kw):
    return pltpu.CompilerParams(vmem_limit_bytes=LIMIT, **kw)


def permute(value, axis, pairs):
    return lax.ppermute(value, axis, pairs)


def swap(value, axis, k):
    return permute(value, axis, [(i, i ^ k) for i in range(lax.axis_size(axis))])


def split(value):
    high = value.astype(BF16)
    return high, (value - high.astype(F32)).astype(BF16)


def dot3(a, b, dims):
    a_high, a_low = split(a)
    b_high, b_low = split(b)

    def one(x, y):
        return lax.dot_general(x, y, (dims, ((), ())), preferred_element_type=F32)

    return one(a_high, b_high) + (one(a_high, b_low) + one(a_low, b_high))


def run_copies(copies, sems):
    started = [pltpu.make_async_copy(a, b, sems.at[i]) for i, (a, b) in enumerate(copies)]
    for copy in started:
        copy.start()
    for copy in started:
        copy.wait()


def aligned(index, step):
    return pl.ds(pl.multiple_of(index * step, step), step)


def cut_columns(value, me, c0, width, parts, after=()):
    lead, total = value.shape[:-1], value.shape[-1]
    step = total // parts

    def kernel(me_ref, src, *rest):
        outs, sems = rest[len(after):-1], rest[-1]
        copies = []
        for k in range(1, parts):
            start = pl.multiple_of((me_ref[0] ^ k) * step + c0, GROUP)
            at = (slice(None),) * len(lead) + (pl.ds(start, width),)
            copies.append((src.at[at], outs[k - 1]))
        run_copies(copies, sems)

    return pl.pallas_call(
        kernel,
        out_shape=[jax.ShapeDtypeStruct(lead + (width,), value.dtype)] * (parts - 1),
        in_specs=[SMEM, ANY] + [ANY] * len(after),
        out_specs=[ANY] * (parts - 1),
        scratch_shapes=[pltpu.SemaphoreType.DMA((parts - 1,))],
        compiler_params=params(),
        name="cut_columns",
    )(me, value, *after)


def join_rows(value, received, me, c0, widths, parts):
    lead, rows, total = value.shape[:-2], value.shape[-2], value.shape[-1]
    step = total // parts
    whole = (slice(None),) * len(lead)

    def kernel(me_ref, src, *rest):
        got, outs, sems = rest[:parts - 1], rest[parts - 1:-1], rest[-1]
        copies = []
        at = 0
        for out, width in zip(outs, widths):
            for k in range(parts):
                dst = out.at[whole + (aligned(me_ref[0] ^ k, rows), slice(None))]
                if k == 0:
                    start = pl.multiple_of(me_ref[0] * step + c0 + at, GROUP)
                    copies.append((src.at[whole + (slice(None), pl.ds(start, width))], dst))
                else:
                    copies.append((got[k - 1].at[whole + (slice(None), pl.ds(at, width))], dst))
            at += width
        run_copies(copies, sems)

    return pl.pallas_call(
        kernel,
        out_shape=[jax.ShapeDtypeStruct(lead + (rows * parts, w), value.dtype) for w in widths],
        in_specs=[SMEM, ANY] + [ANY] * (parts - 1),
        out_specs=[ANY] * len(widths),
        scratch_shapes=[pltpu.SemaphoreType.DMA((parts * len(widths),))],
        compiler_params=params(),
        name="join_rows",
    )(me, value, *received)


def plan_window(devices, hops):
    if devices == 2 * hops + 2 and devices == 8:
        table = np.full((devices, devices), 0, np.int32)
        for z in range(4):
            for y in range(2):
                inner = z in (1, 2)
                far = 3 - z
                cross = far if inner else (2 if z == 0 else 1)
                order = [
                    (z, y), (z ^ 1, y), (far, y), (cross, 1 - y), (z, 1 - y), (z ^ 1, 1 - y),
                    ((3 if z == 1 else 0) if inner else far, 1 - y),
                ]
                for place, (a, b) in enumerate(order):
                    table[2 * z + y, 2 * a + b] = place
        return table, [1, 1, 2, 2, 1, 1, 2]
    offsets = window_offsets(devices, hops)
    table = np.zeros((devices, devices), np.int32)
    for d in range(devices):
        for place, offset in enumerate(offsets):
            table[d, (d + offset) % devices] = place
    return table, [1] * len(offsets)


def window_offsets(devices, hops):
    seen = []
    for offset in range(-hops, hops + 1):
        if offset % devices not in seen:
            seen.append(offset % devices)
    return seen


def gather_window(own, devices, hops):
    if devices == 2 * hops + 2 and devices == 8:
        def lines(pairs):
            return [(2 * a + y, 2 * b + y) for a, b in pairs for y in (0, 1)]

        outer = lines([(0, 1), (1, 0), (2, 3), (3, 2)])
        middle = lines([(1, 2), (2, 1)])
        to_ends = lines([(1, 0), (2, 3)])
        across = [(i, i ^ 1) for i in range(8)]
        across_inner = [(i, i ^ 1) for i in (2, 3, 4, 5)]
        across_ends = [(i, i ^ 1) for i in (0, 1, 6, 7)]
        q1 = permute(own, "blk", outer)
        y1 = permute(own, "blk", across)
        q2 = permute(own, "blk", middle)
        q3 = permute(q1, "blk", middle)
        y2 = permute(q1, "blk", across)
        q5 = permute(y1, "blk", middle)
        q4 = permute(q3, "blk", to_ends)
        y3a = permute(q3, "blk", across_inner)
        q6 = permute(q5, "blk", to_ends)
        y3b = permute(q4, "blk", across_ends)
        return [[own], [q1], [q2, q4], [q5, q6], [y1], [y2], [y3a, y3b]]
    pieces = []
    for offset in window_offsets(devices, hops):
        if offset == 0:
            pieces.append([own])
        else:
            pairs = [((i + offset) % devices, i) for i in range(devices)]
            pieces.append([permute(own, "blk", pairs)])
    return pieces


def apply_kernel(counts, near, groups, orders, places, ends, strips, basis, *rest):
    pieces = rest[:sum(counts)]
    image, partial, raw, window, sems = rest[sum(counts):]
    step = pl.program_id(0)
    rows, width = raw.shape[1], raw.shape[2]
    block = strips.shape[2]

    @pl.when(step == 0)
    def _():
        at = 0
        for place, count in enumerate(counts):
            if count == 1:
                pltpu.make_async_copy(pieces[at], raw.at[place], sems.at[place]).start()
            else:
                @pl.when(ends[0] == 0)
                def _(at=at, place=place):
                    pltpu.make_async_copy(pieces[at], raw.at[place], sems.at[place]).start()

                @pl.when(ends[0] == 1)
                def _(at=at, place=place):
                    pltpu.make_async_copy(pieces[at + 1], raw.at[place], sems.at[place]).start()
            at += count
        for place in range(len(counts)):
            pltpu.make_async_copy(pieces[0], raw.at[place], sems.at[place]).wait()

            def one(i, carry, place=place):
                high, low = split(raw[place, aligned(i, block), :])
                base = (place * (rows // block) + i) * 2
                window[aligned(base, block), :] = high
                window[aligned(base + 1, block), :] = low
                return carry

            lax.fori_loop(0, rows // block, one, 0)
        partial[...] = jnp.zeros_like(partial)

    total = jnp.zeros((2 * block, width), F32)
    for k in range(near):
        high, low = split(strips[0, k])
        left = jnp.concatenate(
            [jnp.concatenate([high, high], 1), jnp.concatenate([low, low], 1)], 0)
        right = window[aligned(places[step, k], 2 * block), :]
        total = total + jnp.dot(left, right, preferred_element_type=F32)
    result = total[:block] + total[block:]
    image[...] = result
    for g in range(groups):
        cols = slice(g * GROUP, (g + 1) * GROUP)
        wide = jnp.concatenate([basis[m, :, cols] for m in range(orders)], 1)
        partial[g] += dot3(result[:, cols], wide, ((0,), (0,)))


def apply(places, ends, strips, basis_rows, pieces, c0, width):
    row_blocks, near, block, _ = strips.shape
    orders = basis_rows.shape[0]
    groups = width // GROUP
    counts = [len(p) for p in pieces]
    flat = [x for p in pieces for x in p]
    rows = flat[0].shape[0]
    column = c0 // width
    return pl.pallas_call(
        functools.partial(apply_kernel, counts, near, groups, orders),
        grid=(row_blocks,),
        out_shape=[
            jax.ShapeDtypeStruct((rows, width), F32),
            jax.ShapeDtypeStruct((groups, GROUP, orders * GROUP), F32),
        ],
        in_specs=[
            SMEM, SMEM,
            pl.BlockSpec((1, near, block, block), lambda i: (i, 0, 0, 0)),
            pl.BlockSpec((orders, block, width), lambda i: (0, i, column)),
        ] + [ANY] * len(flat),
        out_specs=[
            pl.BlockSpec((block, width), lambda i: (i, 0)),
            pl.BlockSpec((groups, GROUP, orders * GROUP), lambda i: (0, 0, 0)),
        ],
        scratch_shapes=[
            pltpu.VMEM((len(counts), rows, width), F32),
            pltpu.VMEM((len(counts) * rows * 2, width), BF16),
            pltpu.SemaphoreType.DMA((len(counts),)),
        ],
        compiler_params=params(),
        cost_estimate=pl.CostEstimate(
            flops=8 * row_blocks * near * block * block * width,
            bytes_accessed=strips.size * 4 + len(counts) * rows * width * 4, transcendentals=0),
        name="apply",
    )(places, ends, strips, basis_rows, *flat)


def project_kernel(groups, orders, image, basis, coeffs_t, residual, gram, coeffs):
    @pl.when(pl.program_id(0) == 0)
    def _():
        gram[...] = jnp.zeros_like(gram)
        for g in range(groups):
            for m in range(orders):
                coeffs[m, g] = coeffs_t[g, :, m * GROUP:(m + 1) * GROUP].T

    for g in range(groups):
        cols = slice(g * GROUP, (g + 1) * GROUP)
        wide = jnp.concatenate([basis[m, :, cols] for m in range(orders)], 1)
        left = image[:, cols] - dot3(wide, coeffs_t[g], ((1,), (1,)))
        residual[:, cols] = left
        gram[g] += dot3(left, left, ((0,), (0,)))


def project(image, basis_rows, coeffs_t, c0, width):
    orders = basis_rows.shape[0]
    groups = width // GROUP
    rows = image.shape[0]
    tile = 256
    column = c0 // width
    return pl.pallas_call(
        functools.partial(project_kernel, groups, orders),
        grid=(rows // tile,),
        out_shape=[
            jax.ShapeDtypeStruct((rows, width), F32),
            jax.ShapeDtypeStruct((groups, GROUP, GROUP), F32),
            jax.ShapeDtypeStruct((orders, groups, GROUP, GROUP), F32),
        ],
        in_specs=[
            pl.BlockSpec((tile, width), lambda i: (i, 0)),
            pl.BlockSpec((orders, tile, width), lambda i: (0, i, column)),
            pl.BlockSpec(coeffs_t.shape, lambda i: (0, 0, 0)),
        ],
        out_specs=[
            pl.BlockSpec((tile, width), lambda i: (i, 0)),
            pl.BlockSpec((groups, GROUP, GROUP), lambda i: (0, 0, 0)),
            pl.BlockSpec((orders, groups, GROUP, GROUP), lambda i: (0, 0, 0, 0)),
        ],
        compiler_params=params(),
        cost_estimate=pl.CostEstimate(
            flops=30 * rows * width * GROUP, bytes_accessed=6 * rows * width * 4,
            transcendentals=0),
        name="project",
    )(image, basis_rows, coeffs_t)


def eliminate(gram):
    count = len(gram)
    order = gram[0].shape[0]
    row_at = lax.broadcasted_iota(jnp.int32, (order, order), 0)
    col_at = lax.broadcasted_iota(jnp.int32, (order, order), 1)
    eye = jnp.where(row_at == col_at, 1.0, 0.0).astype(F32)
    rest = [jnp.concatenate([g, eye], 1) for g in gram]
    done = [[] for _ in gram]
    panel_row = lax.broadcasted_iota(jnp.int32, (PANEL, 1), 0)
    for p0 in range(0, order, PANEL):
        panels = [r[:PANEL] for r in rest]
        for j in range(PANEL):
            for n in range(count):
                panel = panels[n]
                column = panel[:, p0 + j:p0 + j + 1]
                pivot = column[j:j + 1]
                factor = jnp.where(panel_row > j, column / pivot, 0.0)
                panels[n] = panel - factor * panel[j:j + 1]
        for n in range(count):
            panel = panels[n]
            own = slice(p0, p0 + PANEL)
            diagonal = jnp.sum(jnp.where(
                lax.broadcasted_iota(jnp.int32, (PANEL, PANEL), 0)
                == lax.broadcasted_iota(jnp.int32, (PANEL, PANEL), 1),
                panel[:, own], 0.0), axis=1, keepdims=True)
            panel = panel * lax.rsqrt(diagonal)
            done[n].append(panel)
            if p0 + PANEL < order:
                below = panel[:, p0 + PANEL:order]
                rest[n] = rest[n][PANEL:] - lax.dot_general(
                    below, panel, (((0,), (0,)), ((), ())),
                    precision=lax.Precision.HIGHEST, preferred_element_type=F32)
    lowers, inverses = [], []
    for n in range(count):
        upper = jnp.concatenate(done[n], 0)
        lowers.append(jnp.where(row_at >= col_at, upper[:, :order].T, 0.0))
        inverses.append(upper[:, order:])
    return lowers, inverses


def finish_kernel(groups, parts, me, gram, residual, *outs):
    lowers, inverses = eliminate([gram[g] for g in range(groups)])
    rows = residual.shape[0] // parts
    for k in range(parts):
        for g in range(groups):
            cols = slice(g * GROUP, (g + 1) * GROUP)
            left = residual[aligned(me[0] ^ k, rows), cols]
            outs[k][:rows, cols] = dot3(left, inverses[g], ((1,), (1,)))
            outs[k][rows:, cols] = lowers[g]


def finish(me, gram, residual, parts):
    groups = gram.shape[0]
    rows, width = residual.shape
    shape = jax.ShapeDtypeStruct((rows // parts + GROUP, width), F32)
    return pl.pallas_call(
        functools.partial(finish_kernel, groups, parts),
        out_shape=[shape] * parts,
        in_specs=[SMEM, VMEM, VMEM],
        out_specs=[VMEM] * parts,
        compiler_params=params(),
        cost_estimate=pl.CostEstimate(
            flops=6 * rows * width * GROUP, bytes_accessed=4 * rows * width * 4,
            transcendentals=0),
        name="finish",
    )(me, gram, residual)


def collect(me, blocks, coeffs, chunks, shapes, parts):
    new_shape, coeffs_shape, factor_shape = shapes
    rows = new_shape[0]
    step = new_shape[1] // parts
    count = len(chunks)
    per_part = step // GROUP

    def kernel(me_ref, *rest):
        new_in, coeffs_in = rest[:count * parts], rest[count * parts:2 * count * parts]
        new_out, coeffs_out, factor_out, sems = rest[2 * count * parts:]
        copies = []
        for c, (g0, groups) in enumerate(chunks):
            for k in range(parts):
                src = new_in[c * parts + k]
                at = me_ref[0] ^ k
                start = pl.multiple_of(at * step + g0 * GROUP, GROUP)
                copies.append((src.at[pl.ds(0, rows), :],
                               new_out.at[:, pl.ds(start, groups * GROUP)]))
                copies.append((coeffs_in[c * parts + k],
                               coeffs_out.at[:, pl.ds(at * per_part + g0, groups)]))
                for g in range(groups):
                    copies.append((src.at[pl.ds(rows, GROUP), pl.ds(g * GROUP, GROUP)],
                                   factor_out.at[at * per_part + g0 + g]))
        run_copies(copies, sems)

    total = sum(parts * (2 + groups) for _, groups in chunks)
    return pl.pallas_call(
        kernel,
        out_shape=[jax.ShapeDtypeStruct(s, F32) for s in shapes],
        in_specs=[SMEM] + [ANY] * (2 * count * parts),
        out_specs=[ANY] * 3,
        scratch_shapes=[pltpu.SemaphoreType.DMA((total,))],
        compiler_params=params(),
        name="collect",
    )(me, *[x for c in blocks for x in c], *[x for c in coeffs for x in c])


def sum_blk(value):
    k = 1
    while k < lax.axis_size("blk"):
        value = value + swap(value, "blk", k)
        k *= 2
    return value


def plan_chunks(groups):
    chunks, at = [], 0
    for size in CHUNKS if sum(CHUNKS) == groups else (1,) * groups:
        chunks.append((at, size))
        at += size
    return chunks


def local(strips, near_cols, vector_block, basis):
    local_blocks = strips.shape[0]
    devices = lax.axis_size("blk")
    parts = lax.axis_size("rhs")
    hops = -(-BAND // local_blocks)
    rows, total = vector_block.shape
    step = total // parts
    groups = step // GROUP
    orders = basis.shape[0]
    chunks = plan_chunks(groups)
    me = lax.axis_index("rhs").astype(jnp.int32).reshape(1)
    blk = lax.axis_index("blk")

    table, _ = plan_window(devices, hops)
    row = jnp.asarray(table)[blk]
    places = row[near_cols // local_blocks] * local_blocks + near_cols % local_blocks
    ends = jnp.where((blk < 2) | (blk >= devices - 2), 1, 0).astype(jnp.int32).reshape(1)

    def row_form(value, c0, widths, after=()):
        sent = cut_columns(value, me, c0, sum(widths), parts, after)
        got = [swap(s, "rhs", k + 1) for k, s in enumerate(sent)]
        return join_rows(value, got, me, c0, widths, parts)

    first = chunks[0][1] * GROUP
    own = row_form(vector_block, 0, [first])
    if len(chunks) > 1:
        own = own + row_form(vector_block, first, [n * GROUP for _, n in chunks[1:]])
    basis_rows, = row_form(basis, 0, [step], after=(own[-1],))

    blocks, all_coeffs = [], []
    for (g0, count), mine in zip(chunks, own):
        width = count * GROUP
        pieces = gather_window(mine, devices, hops)
        image, partial = apply(places, ends, strips, basis_rows, pieces, g0 * GROUP, width)
        coeffs_t = sum_blk(partial)
        residual, gram, coeffs = project(image, basis_rows, coeffs_t, g0 * GROUP, width)
        gram = sum_blk(gram)
        all_coeffs.append([coeffs] + [swap(coeffs, "rhs", k) for k in range(1, parts)])
        out = finish(me, gram, residual, parts)
        blocks.append([out[0]] + [swap(out[k], "rhs", k) for k in range(1, parts)])

    shapes = [(rows, total), (orders, total // GROUP, GROUP, GROUP), (total // GROUP, GROUP, GROUP)]
    return tuple(collect(me, blocks, all_coeffs, chunks, shapes, parts))


def solution(mesh):
    placed = (
        P("blk", None, None, None),
        P("blk", None),
        P(("blk", "rhs"), None),
        P(None, ("blk", "rhs"), None),
    )
    return jax.shard_map(
        local,
        mesh=mesh,
        in_specs=placed,
        out_specs=(P(("blk", "rhs"), None), P(), P()),
        check_vma=False,
    )
```

```python
import functools

import jax
import jax.numpy as jnp
import numpy as np
from jax import lax
from jax.experimental import pallas as pl
from jax.experimental.pallas import tpu as pltpu
from jax.sharding import PartitionSpec as P

GROUP = 128
BAND = 24
PANEL = 32
HALVED = 128

F32 = jnp.float32
BF16 = jnp.bfloat16
ANY = pl.BlockSpec(memory_space=pl.ANY)
SMEM = pl.BlockSpec(memory_space=pltpu.SMEM)
VMEM = pl.BlockSpec(memory_space=pltpu.VMEM)
LIMIT = 50 * 1024 * 1024


def params(**kw):
    return pltpu.CompilerParams(vmem_limit_bytes=LIMIT, **kw)


def pairs_of(axis, k):
    return [(i, i ^ k) for i in range(lax.axis_size(axis))]


def swap(value, axis, k):
    return lax.ppermute(value, axis, pairs_of(axis, k))


def split(value):
    high = value.astype(BF16)
    return high, (value - high.astype(F32)).astype(BF16)


def dot3(a, b, dims):
    a_high, a_low = split(a)
    b_high, b_low = split(b)

    def one(x, y):
        return lax.dot_general(x, y, (dims, ((), ())), preferred_element_type=F32)

    return one(a_high, b_high) + (one(a_high, b_low) + one(a_low, b_high))


def aligned(index, step):
    return pl.ds(pl.multiple_of(index * step, step), step)


def column_spec(value, layer, parts, k):
    rows, step = value.shape[1], value.shape[2] // parts
    return pl.BlockSpec((1, rows, step), lambda i, me: (layer + i, 0, me[0] ^ k))


def layer_spec(rows, width):
    return pl.BlockSpec((1, rows, width), lambda i, me: (i, 0, 0))


def cut_columns(value, layer, layers, me, ks, c0, width, parts, after=()):
    rows = value.shape[1]

    def kernel(me_ref, *refs):
        for src, dst in zip(refs, refs[-len(ks):]):
            dst[...] = src[:, :, c0:c0 + width]

    return pl.pallas_call(
        kernel,
        grid_spec=pltpu.PrefetchScalarGridSpec(
            num_scalar_prefetch=1,
            grid=(layers,),
            in_specs=[column_spec(value, layer, parts, k) for k in ks] + [ANY] * len(after),
            out_specs=[layer_spec(rows, width)] * len(ks),
        ),
        out_shape=[jax.ShapeDtypeStruct((layers, rows, width), value.dtype)] * len(ks),
        compiler_params=params(),
        name="cut_columns",
    )(me, *[value] * len(ks), *after)


def join_rows(value, layer, layers, received, me, c0, widths, parts):
    rows = value.shape[1]
    width = sum(widths)

    def kernel(me_ref, *refs):
        for k in range(parts):
            at = c0 if k == 0 else 0
            for out, w in zip(refs[parts:], widths):
                out[0, aligned(me_ref[0] ^ k, rows), :] = refs[k][0, :, at:at + w]
                at += w

    return pl.pallas_call(
        kernel,
        grid_spec=pltpu.PrefetchScalarGridSpec(
            num_scalar_prefetch=1,
            grid=(layers,),
            in_specs=[column_spec(value, layer, parts, 0)]
            + [layer_spec(rows, width)] * (parts - 1),
            out_specs=[layer_spec(rows * parts, w) for w in widths],
        ),
        out_shape=[jax.ShapeDtypeStruct((layers, rows * parts, w), value.dtype) for w in widths],
        compiler_params=params(),
        name="join_rows",
    )(me, value, *received)


def two_lines(devices, hops):
    return devices == 8 and devices == 2 * hops + 2


def window_offsets(devices, hops):
    seen = []
    for offset in range(-hops, hops + 1):
        if offset % devices not in seen:
            seen.append(offset % devices)
    return sorted(seen, key=lambda offset: min(offset, devices - offset))


def plan_window(devices, hops):
    table = np.zeros((devices, devices), np.int32)
    if two_lines(devices, hops):
        for z in range(4):
            for y in range(2):
                inner, far, back = z in (1, 2), 3 - z, 1 - y
                places = [
                    (z, y), (z ^ 1, y), (z, back), (z ^ 1, back), (far, back if inner else y),
                    (far, y) if inner else (2 if z == 0 else 1, back),
                    (3 if z == 1 else 0, back) if inner else (far, back),
                ]
                for place, (a, b) in enumerate(places):
                    table[2 * z + y, 2 * a + b] = place
        return table
    for d in range(devices):
        for place, offset in enumerate(window_offsets(devices, hops)):
            table[d, (d + offset) % devices] = place
    return table


def relay_plan():
    def lines(pairs):
        return [(2 * a + y, 2 * b + y) for a, b in pairs for y in (0, 1)]

    outer = lines([(0, 1), (1, 0), (2, 3), (3, 2)])
    middle = lines([(1, 2), (2, 1)])
    to_ends = lines([(1, 0), (2, 3)])
    across = [(i, i ^ 1) for i in range(8)]
    across_inner = [(i, i ^ 1) for i in (2, 3, 4, 5)]
    across_ends = [(i, i ^ 1) for i in (0, 1, 6, 7)]
    return {
        "q1": ("own", outer), "y1": ("own", across), "q2": ("own", middle),
        "q3": ("q1", middle), "y2": ("q1", across), "q5": ("y1", middle),
        "q4": ("q3", to_ends), "y3a": ("q3", across_inner),
        "q6": ("q5", to_ends), "y3b": ("q4", across_ends),
    }


ROUNDS = (
    (("q1", 0), ("y1", 0), ("q2", 0)),
    (("q3", 0), ("y2", 0), ("q1", 1)),
    (("q5", 0), ("q4", 0), ("y1", 1)),
    (("q6", 0), ("y3a", 0), ("y3b", 0), ("q3", 1)),
    (("q5", 1), ("q4", 1), ("y2", 1)),
    (("q6", 1), ("y3a", 1), ("y3b", 1), ("q2", 1)),
)
PLACES = (("own",), ("q1",), ("y1",), ("y2",), ("q5", "q4"), ("q2", "q6"), ("y3a", "y3b"))


def load_window(pieces, counts, ends, raw, window, sems, block):
    rows = raw.shape[1]
    at = 0
    for place, count in enumerate(counts):
        for end in range(count):
            def fetch(at=at, place=place, end=end):
                pltpu.make_async_copy(pieces[at + end], raw.at[place], sems.at[place]).start()

            if count == 1:
                fetch()
            else:
                pl.when(ends[0] == end)(fetch)
        at += count
    for place in range(len(counts)):
        pltpu.make_async_copy(pieces[0], raw.at[place], sems.at[place]).wait()

        def one(i, carry, place=place):
            high, low = split(raw[place, aligned(i, block), :])
            base = (place * (rows // block) + i) * 2
            window[aligned(base, block), :] = high
            window[aligned(base + 1, block), :] = low
            return carry

        lax.fori_loop(0, rows // block, one, 0)


def four_terms(strip):
    high, low = split(strip)
    return jnp.concatenate(
        [jnp.concatenate([high, high], 1), jnp.concatenate([low, low], 1)], 0)


def apply_kernel(counts, near, places, ends, strips, *rest):
    pieces = rest[:sum(counts)]
    image, raw, window, sems = rest[sum(counts):]
    step = pl.program_id(0)
    block = strips.shape[2]

    @pl.when(step == 0)
    def _():
        load_window(pieces, counts, ends, raw, window, sems, block)

    total = jnp.zeros((2 * block, raw.shape[2]), F32)
    for k in range(near):
        right = window[aligned(places[step, k], 2 * block), :]
        total = total + jnp.dot(four_terms(strips[0, k]), right, preferred_element_type=F32)
    image[...] = total[:block] + total[block:]


def group_specs(basis_rows, tile, g0, groups):
    specs, arrays = [], []
    for g in range(g0, g0 + groups):
        for value in basis_rows:
            for m in range(value.shape[0]):
                specs.append(pl.BlockSpec((1, tile, GROUP), lambda i, m=m, g=g: (m, i, g)))
                arrays.append(value)
    return specs, arrays


def apply(places, ends, strips, pieces):
    row_blocks, near, block, _ = strips.shape
    rows, width = pieces[0][0].shape
    counts = [len(p) for p in pieces]
    flat = [x for p in pieces for x in p]
    return pl.pallas_call(
        functools.partial(apply_kernel, counts, near),
        grid=(row_blocks,),
        out_shape=jax.ShapeDtypeStruct((rows, width), F32),
        in_specs=[SMEM, SMEM, pl.BlockSpec((1, near, block, block), lambda i: (i, 0, 0, 0))]
        + [ANY] * len(flat),
        out_specs=pl.BlockSpec((block, width), lambda i: (i, 0)),
        scratch_shapes=[
            pltpu.VMEM((len(counts), rows, width), F32),
            pltpu.VMEM((len(counts) * rows * 2, width), BF16),
            pltpu.SemaphoreType.DMA((len(counts),)),
        ],
        compiler_params=params(),
        cost_estimate=pl.CostEstimate(
            flops=8 * row_blocks * near * block * block * width,
            bytes_accessed=strips.size * 4 + 8 * rows * width * 4, transcendentals=0),
        name="apply",
    )(places, ends, strips, *flat)


def inner_kernel(orders, image, *rest):
    basis, partial = rest[:-1], rest[-1]

    @pl.when(pl.program_id(0) == 0)
    def _():
        partial[...] = jnp.zeros_like(partial)

    for g in range(partial.shape[0]):
        cols = slice(g * GROUP, (g + 1) * GROUP)
        wide = jnp.concatenate([basis[g * orders + m][0] for m in range(orders)], 1)
        partial[g] += dot3(image[:, cols], wide, ((0,), (0,)))


def inner(image, at, basis_rows, g0, groups):
    rows, width = image.shape[0], groups * GROUP
    orders = sum(x.shape[0] for x in basis_rows)
    tile = rows // 4
    specs, arrays = group_specs(basis_rows, tile, g0, groups)
    shape = (groups, GROUP, orders * GROUP)
    return pl.pallas_call(
        functools.partial(inner_kernel, orders),
        grid=(rows // tile,),
        out_shape=jax.ShapeDtypeStruct(shape, F32),
        in_specs=[pl.BlockSpec((tile, width), lambda i: (i, at // groups))] + specs,
        out_specs=pl.BlockSpec(shape, lambda i: (0, 0, 0)),
        compiler_params=params(),
        cost_estimate=pl.CostEstimate(
            flops=24 * rows * width * GROUP, bytes_accessed=5 * rows * width * 4,
            transcendentals=0),
        name="inner",
    )(image, *arrays)


def project_kernel(orders, image, coeffs_t, *rest):
    groups = coeffs_t.shape[0]
    basis, (residual, gram, coeffs) = rest[:groups * orders], rest[groups * orders:]

    @pl.when(pl.program_id(0) == 0)
    def _():
        gram[...] = jnp.zeros_like(gram)
        for g in range(groups):
            for m in range(orders):
                coeffs[m, g] = coeffs_t[g, :, m * GROUP:(m + 1) * GROUP].T

    for g in range(groups):
        cols = slice(g * GROUP, (g + 1) * GROUP)
        wide = jnp.concatenate([basis[g * orders + m][0] for m in range(orders)], 1)
        left = image[:, cols] - dot3(wide, coeffs_t[g], ((1,), (1,)))
        residual[:, cols] = left
        gram[g] += dot3(left, left, ((0,), (0,)))


def project(image, at, basis_rows, coeffs_t, g0, groups):
    orders = sum(x.shape[0] for x in basis_rows)
    rows, width = image.shape[0], groups * GROUP
    tile = rows // 4
    specs, arrays = group_specs(basis_rows, tile, g0, groups)
    return pl.pallas_call(
        functools.partial(project_kernel, orders),
        grid=(rows // tile,),
        out_shape=[
            jax.ShapeDtypeStruct((rows, width), F32),
            jax.ShapeDtypeStruct((groups, GROUP, GROUP), F32),
            jax.ShapeDtypeStruct((orders, groups, GROUP, GROUP), F32),
        ],
        in_specs=[
            pl.BlockSpec((tile, width), lambda i: (i, at // groups)),
            pl.BlockSpec(coeffs_t.shape, lambda i: (0, 0, 0)),
        ] + specs,
        out_specs=[
            pl.BlockSpec((tile, width), lambda i: (i, 0)),
            pl.BlockSpec((groups, GROUP, GROUP), lambda i: (0, 0, 0)),
            pl.BlockSpec((orders, groups, GROUP, GROUP), lambda i: (0, 0, 0, 0)),
        ],
        compiler_params=params(),
        cost_estimate=pl.CostEstimate(
            flops=30 * rows * width * GROUP, bytes_accessed=6 * rows * width * 4,
            transcendentals=0),
        name="project",
    )(image, coeffs_t, *arrays)


def eliminate(gram):
    count = len(gram)
    order = gram[0].shape[0]
    row_at = lax.broadcasted_iota(jnp.int32, (order, order), 0)
    col_at = lax.broadcasted_iota(jnp.int32, (order, order), 1)
    eye = jnp.where(row_at == col_at, 1.0, 0.0).astype(F32)
    rest = [jnp.concatenate([g, eye], 1) for g in gram]
    done = [[] for _ in gram]
    panel_row = lax.broadcasted_iota(jnp.int32, (PANEL, 1), 0)
    for p0 in range(0, order, PANEL):
        panels = [r[:PANEL] for r in rest]
        for j in range(PANEL):
            for n in range(count):
                panel = panels[n]
                column = panel[:, p0 + j:p0 + j + 1]
                pivot = column[j:j + 1]
                factor = jnp.where(panel_row > j, column / pivot, 0.0)
                panels[n] = panel - factor * panel[j:j + 1]
        for n in range(count):
            panel = panels[n]
            own = slice(p0, p0 + PANEL)
            diagonal = jnp.sum(jnp.where(
                lax.broadcasted_iota(jnp.int32, (PANEL, PANEL), 0)
                == lax.broadcasted_iota(jnp.int32, (PANEL, PANEL), 1),
                panel[:, own], 0.0), axis=1, keepdims=True)
            panel = panel * lax.rsqrt(diagonal)
            done[n].append(panel)
            if p0 + PANEL < order:
                below = panel[:, p0 + PANEL:order]
                rest[n] = rest[n][PANEL:] - lax.dot_general(
                    below, panel, (((0,), (0,)), ((), ())),
                    precision=lax.Precision.HIGHEST, preferred_element_type=F32)
    lowers, inverses = [], []
    for n in range(count):
        upper = jnp.concatenate(done[n], 0)
        lowers.append(jnp.where(row_at >= col_at, upper[:, :order].T, 0.0))
        inverses.append(upper[:, order:])
    return lowers, inverses


def finish_kernel(groups, parts, me, gram, residual, *outs):
    lowers, inverses = eliminate([gram[g] for g in range(groups)])
    rows = residual.shape[0] // parts
    for k in range(parts):
        for g in range(groups):
            cols = slice(g * GROUP, (g + 1) * GROUP)
            left = residual[aligned(me[0] ^ k, rows), cols]
            outs[k][:rows, cols] = dot3(left, inverses[g], ((1,), (1,)))
            outs[k][rows:, cols] = lowers[g]


def finish(me, gram, residual, parts):
    groups = gram.shape[0]
    rows, width = residual.shape
    shape = jax.ShapeDtypeStruct((rows // parts + GROUP, width), F32)
    return pl.pallas_call(
        functools.partial(finish_kernel, groups, parts),
        out_shape=[shape] * parts,
        in_specs=[SMEM, VMEM, VMEM],
        out_specs=[VMEM] * parts,
        compiler_params=params(),
        cost_estimate=pl.CostEstimate(
            flops=6 * rows * width * GROUP, bytes_accessed=4 * rows * width * 4,
            transcendentals=0),
        name="finish",
    )(me, gram, residual)


def collect_blocks(me, blocks, chunks, new_shape, factor_shape, parts):
    rows = new_shape[0]
    step = new_shape[1] // parts
    per_part = step // GROUP

    def kernel(me_ref, *refs):
        new_out, factor_out = refs[-2:]
        for c, (g0, groups) in enumerate(chunks):
            for k in range(parts):
                src = refs[c * parts + k]
                at = me_ref[0] ^ k
                for g in range(groups):
                    cols = slice(g * GROUP, (g + 1) * GROUP)
                    group = at * per_part + g0 + g
                    new_out[:, aligned(group, GROUP)] = src[:rows, cols]
                    factor_out[group] = src[rows:, cols]

    return pl.pallas_call(
        kernel,
        out_shape=[jax.ShapeDtypeStruct(new_shape, F32), jax.ShapeDtypeStruct(factor_shape, F32)],
        in_specs=[SMEM] + [VMEM] * (len(chunks) * parts),
        out_specs=[VMEM] * 2,
        compiler_params=params(),
        name="collect_blocks",
    )(me, *[x for c in blocks for x in c])


def collect_coeffs(me, coeffs, chunks, shape, parts):
    per_part = shape[1] // parts

    def kernel(me_ref, *refs):
        for c, (g0, groups) in enumerate(chunks):
            for k in range(parts):
                for g in range(groups):
                    refs[-1][:, (me_ref[0] ^ k) * per_part + g0 + g] = refs[c * parts + k][:, g]

    return pl.pallas_call(
        kernel,
        out_shape=jax.ShapeDtypeStruct(shape, F32),
        in_specs=[SMEM] + [VMEM] * (len(chunks) * parts),
        out_specs=VMEM,
        compiler_params=params(),
        name="collect_coeffs",
    )(me, *[x for c in coeffs for x in c])


def sum_blk(value):
    devices = lax.axis_size("blk")
    half = value.shape[0] // 2
    side = lax.axis_index("blk") % 2
    long = value.shape[0] > HALVED
    if long:
        kept = lax.dynamic_slice_in_dim(value, side * half, half, 0)
        sent = lax.dynamic_slice_in_dim(value, (1 - side) * half, half, 0)
        value = kept + swap(sent, "blk", 1)
    k = 2 if long else 1
    while k < devices:
        value = value + swap(value, "blk", k)
        k *= 2
    if long:
        other = swap(value, "blk", 1)
        value = jnp.concatenate(
            [jnp.where(side == 0, value, other), jnp.where(side == 0, other, value)], 0)
    return value


def sum_groups(value):
    return sum_blk(value.reshape(-1, value.shape[-1])).reshape(value.shape)


def local(strips, near_cols, vector_block, basis):
    local_blocks = strips.shape[0]
    devices = lax.axis_size("blk")
    parts = lax.axis_size("rhs")
    hops = -(-BAND // local_blocks)
    rows, total = vector_block.shape
    step = total // parts
    groups = step // GROUP
    orders = basis.shape[0]
    chunks = [(0, groups - groups // 2), (groups - groups // 2, groups // 2)]
    chunks = [chunk for chunk in chunks if chunk[1]]
    me = lax.axis_index("rhs").astype(jnp.int32).reshape(1)
    blk = lax.axis_index("blk")
    others = list(range(1, parts))
    relayed = two_lines(devices, hops) and len(chunks) == 2

    table = plan_window(devices, hops)
    place = jnp.asarray(table)[blk][near_cols // local_blocks]
    inside = near_cols % local_blocks
    places = place * local_blocks + inside
    ends = jnp.where((blk < 2) | (blk >= devices - 2), 1, 0).astype(jnp.int32).reshape(1)

    vector = vector_block[None]
    half = -(-orders // 2)
    values = {}

    def send(key):
        kind, at, k = key
        values[key] = swap(values["cut", kind, at, k], "rhs", k)

    def cut(kind, at, value, layer, layers, c0, width):
        for k, x in zip(others, cut_columns(
                value, layer, layers, me, others, c0, width, parts)):
            values["cut", kind, at, k] = x

    def join(kind, at, value, layer, layers, c0, width):
        got = [values[kind, at, k] for k in others]
        return join_rows(value, layer, layers, got, me, c0, [width], parts)[0]

    def own_rows(c):
        c0, width = chunks[c][0] * GROUP, chunks[c][1] * GROUP
        values["own", c] = join("v", c, vector, 0, 1, c0, width)[0]

    for c, (g0, n) in enumerate(chunks):
        cut("v", c, vector, 0, 1, g0 * GROUP, n * GROUP)
    layers = [(m, min(half, orders - m)) for m in range(0, orders, half)]
    for h, (m, n) in enumerate(layers):
        cut("b", h, basis, m, n, 0, step)

    def barrier(flying=()):
        keys = [key for key in values if key not in flying]
        for key, x in zip(keys, lax.optimization_barrier(tuple(values[k] for k in keys))):
            values[key] = x

    def window(c):
        return [[values[n, c] for n in alternatives] for alternatives in PLACES]

    for k in others:
        send(("v", 0, k))
    own_rows(0)
    if relayed:
        plan = relay_plan()
        beside = {}
        for h in range(len(layers)):
            for k in others:
                beside.setdefault(1 + h if k == 1 else 2 * h + k - 1, []).append(("b", h, k))
        for r, relays in enumerate(ROUNDS):
            for name, c in relays:
                source, pairs = plan[name]
                values[name, c] = lax.ppermute(values[source, c], "blk", pairs)
            if r == 0:
                for k in others:
                    send(("v", 1, k))
                own_rows(1)
            flying = beside.get(r, ())
            for key in flying:
                send(key)
            if r == 4:
                values["image", 0] = apply(places, ends, strips, window(0))
            if r == 5:
                basis_rows = [join("b", h, basis, m, n, 0, step) for h, (m, n) in enumerate(layers)]
                for h, x in enumerate(basis_rows):
                    values["basis", h] = x
                values["partial", 0] = inner(values["image", 0], 0, basis_rows, *chunks[0])
            barrier(flying if True else ())
        basis_rows = [values["basis", h] for h in range(len(layers))]
        values["image", 1] = apply(places, ends, strips, window(1))
    else:
        for c in range(1, len(chunks)):
            for k in others:
                send(("v", c, k))
            own_rows(c)
        for h in range(len(layers)):
            for k in others:
                send(("b", h, k))
        basis_rows = [join("b", h, basis, m, n, 0, step) for h, (m, n) in enumerate(layers)]
        for c in range(len(chunks)):
            pieces = []
            for offset in window_offsets(devices, hops):
                pairs = [((i + offset) % devices, i) for i in range(devices)]
                own = values["own", c]
                pieces.append([lax.ppermute(own, "blk", pairs) if offset else own])
            values["image", c] = apply(places, ends, strips, pieces)

    tail = [(0, 0, *chunks[0])]
    if len(chunks) == 2:
        tail += [(1, 0, *chunks[1])] if True else [
            (1, g, chunks[1][0] + g, 1) for g in range(chunks[1][1])]
    blocks, all_coeffs, made = [], [], []
    for c, at, g0, n in tail:
        if (c, at) == (0, 0) and ("partial", 0) in values:
            part = values["partial", 0]
        else:
            part = inner(values["image", c], at, basis_rows, g0, n)
        made.append(project(values["image", c], at, basis_rows, sum_groups(part), g0, n))
    for (c, at, g0, n), (residual, gram, coeffs) in zip(tail, made):
        across = [swap(coeffs, "rhs", k) for k in others if k > 1 and not k & 1]
        both = [coeffs] + across
        pair = [swap(x, "rhs", 1) for x in both]
        all_coeffs.append([x for two in zip(both, pair) for x in two])
        out = finish(me, sum_groups(gram), residual, parts)
        blocks.append([out[0]] + [swap(out[k], "rhs", k) for k in others])
    chunks = [(g0, n) for _, _, g0, n in tail]

    coeffs = collect_coeffs(
        me, all_coeffs, chunks, (orders, total // GROUP, GROUP, GROUP), parts)
    new_block, factor = collect_blocks(
        me, blocks, chunks, (rows, total), (total // GROUP, GROUP, GROUP), parts)
    return new_block, coeffs, factor


def solution(mesh):
    placed = (
        P("blk", None, None, None),
        P("blk", None),
        P(("blk", "rhs"), None),
        P(None, ("blk", "rhs"), None),
    )
    return jax.shard_map(
        local,
        mesh=mesh,
        in_specs=placed,
        out_specs=(P(("blk", "rhs"), None), P(), P()),
        check_vma=False,
    )
```

```python
import functools

import jax
import jax.numpy as jnp
import numpy as np
from jax import lax
from jax.experimental import pallas as pl
from jax.experimental.pallas import tpu as pltpu
from jax.sharding import PartitionSpec as P

GROUP = 128
BAND = 24
PANEL = 32
AHEAD = 8
TOGETHER = 4
HALVED = 128

F32 = jnp.float32
BF16 = jnp.bfloat16
ANY = pl.BlockSpec(memory_space=pl.ANY)
SMEM = pl.BlockSpec(memory_space=pltpu.SMEM)
VMEM = pl.BlockSpec(memory_space=pltpu.VMEM)
LIMIT = 50 * 1024 * 1024


def params(**kw):
    return pltpu.CompilerParams(vmem_limit_bytes=LIMIT, **kw)


def pairs_of(axis, k):
    return [(i, i ^ k) for i in range(lax.axis_size(axis))]


def swap(value, axis, k):
    return lax.ppermute(value, axis, pairs_of(axis, k))


def split(value):
    high = value.astype(BF16)
    return high, (value - high.astype(F32)).astype(BF16)


def dot3(a, b, dims):
    return dot3_parts(split(a), split(b), dims)


def dot3_parts(a, b, dims):
    (a_high, a_low), (b_high, b_low) = a, b

    def one(x, y):
        return lax.dot_general(x, y, (dims, ((), ())), preferred_element_type=F32)

    return one(a_high, b_high) + (one(a_high, b_low) + one(a_low, b_high))


def aligned(index, step):
    return pl.ds(pl.multiple_of(index * step, step), step)


def column_spec(value, layer, parts, k):
    rows, step = value.shape[1], value.shape[2] // parts
    return pl.BlockSpec((1, rows, step), lambda i, me: (layer + i, 0, me[0] ^ k))


def layer_spec(rows, width):
    return pl.BlockSpec((1, rows, width), lambda i, me: (i, 0, 0))


def cut_columns(value, layer, layers, me, ks, c0, width, parts, after=()):
    rows = value.shape[1]

    def kernel(me_ref, *refs):
        for src, dst in zip(refs, refs[-len(ks):]):
            dst[...] = src[:, :, c0:c0 + width]

    return pl.pallas_call(
        kernel,
        grid_spec=pltpu.PrefetchScalarGridSpec(
            num_scalar_prefetch=1,
            grid=(layers,),
            in_specs=[column_spec(value, layer, parts, k) for k in ks] + [ANY] * len(after),
            out_specs=[layer_spec(rows, width)] * len(ks),
        ),
        out_shape=[jax.ShapeDtypeStruct((layers, rows, width), value.dtype)] * len(ks),
        compiler_params=params(),
        name="cut_columns",
    )(me, *[value] * len(ks), *after)


def join_rows(value, layer, layers, received, me, c0, width, parts, halves=False):
    rows = value.shape[1]
    types = [BF16, BF16] if halves else [value.dtype]

    def kernel(me_ref, *refs):
        for k in range(parts):
            at = c0 if k == 0 else 0
            piece = refs[k][0, :, at:at + width]
            for out, x in zip(refs[parts:], split(piece) if halves else [piece]):
                out[0, aligned(me_ref[0] ^ k, rows), :] = x

    return pl.pallas_call(
        kernel,
        grid_spec=pltpu.PrefetchScalarGridSpec(
            num_scalar_prefetch=1,
            grid=(layers,),
            in_specs=[column_spec(value, layer, parts, 0)]
            + [layer_spec(rows, width)] * (parts - 1),
            out_specs=[layer_spec(rows * parts, width)] * len(types),
        ),
        out_shape=[jax.ShapeDtypeStruct((layers, rows * parts, width), t) for t in types],
        compiler_params=params(),
        name="join_rows",
    )(me, value, *received)


def two_lines(devices, hops):
    return devices == 8 and devices == 2 * hops + 2


def window_offsets(devices, hops):
    seen = []
    for offset in range(-hops, hops + 1):
        if offset % devices not in seen:
            seen.append(offset % devices)
    return sorted(seen, key=lambda offset: min(offset, devices - offset))


def plan_window(devices, hops):
    table = np.zeros((devices, devices), np.int32)
    if two_lines(devices, hops):
        for z in range(4):
            for y in range(2):
                inner, far, back = z in (1, 2), 3 - z, 1 - y
                places = [
                    (z, y), (z ^ 1, y), (z, back), (z ^ 1, back), (far, back if inner else y),
                    (far, y) if inner else (2 if z == 0 else 1, back),
                    (3 if z == 1 else 0, back) if inner else (far, back),
                ]
                for place, (a, b) in enumerate(places):
                    table[2 * z + y, 2 * a + b] = place
        return table
    for d in range(devices):
        for place, offset in enumerate(window_offsets(devices, hops)):
            table[d, (d + offset) % devices] = place
    return table


def relay_plan():
    def lines(pairs):
        return [(2 * a + y, 2 * b + y) for a, b in pairs for y in (0, 1)]

    outer = lines([(0, 1), (1, 0), (2, 3), (3, 2)])
    middle = lines([(1, 2), (2, 1)])
    to_ends = lines([(1, 0), (2, 3)])
    across = [(i, i ^ 1) for i in range(8)]
    return {
        "q1": ("own", outer), "y1": ("own", across), "q2": ("own", middle),
        "q3": ("q1", middle), "y2": ("q1", across), "q5": ("y1", middle),
        "q4": ("q3", to_ends), "q6": ("q5", to_ends),
        "y3": (("q3", "q4"), across),
    }


ROUNDS = (
    (("q1", 0), ("y1", 0), ("q2", 0)),
    (("q3", 0), ("y2", 0), ("q1", 1)),
    (("q5", 0), ("q4", 0), ("y1", 1)),
    (("q6", 0), ("y3", 0), ("q3", 1)),
    (("q5", 1), ("q4", 1), ("y2", 1)),
    (("q6", 1), ("y3", 1), ("q2", 1)),
)
PLACES = (("own",), ("q1",), ("y1",), ("y2",), ("q5", "q4"), ("q2", "q6"), ("y3",))


def load_window(pieces, counts, ends, raw, window, sems, block):
    rows = raw.shape[1]
    at = 0
    for place, count in enumerate(counts):
        for end in range(count):
            def fetch(at=at, place=place, end=end):
                pltpu.make_async_copy(pieces[at + end], raw.at[place], sems.at[place]).start()

            if count == 1:
                fetch()
            else:
                pl.when(ends[0] == end)(fetch)
        at += count
    for place in range(len(counts)):
        pltpu.make_async_copy(pieces[0], raw.at[place], sems.at[place]).wait()

        def one(i, carry, place=place):
            high, low = split(raw[place, aligned(i, block), :])
            base = (place * (rows // block) + i) * 2
            window[aligned(base, block), :] = high
            window[aligned(base + 1, block), :] = low
            return carry

        lax.fori_loop(0, rows // block, one, 0)


def four_terms(strip):
    high, low = split(strip)
    return jnp.concatenate(
        [jnp.concatenate([high, high], 1), jnp.concatenate([low, low], 1)], 0)


def apply_kernel(counts, near, places, ends, strips, *rest):
    pieces = rest[:sum(counts)]
    image, raw, window, sems = rest[sum(counts):]
    step = pl.program_id(0)
    block = strips.shape[2]

    @pl.when(step == 0)
    def _():
        load_window(pieces, counts, ends, raw, window, sems, block)
        window[len(counts) * raw.shape[1] * 2:, :] = jnp.zeros((2 * block, raw.shape[2]), BF16)

    total = jnp.zeros((2 * block, raw.shape[2]), F32)
    for k in range(near):
        right = window[aligned(places[step, k], 2 * block), :]
        total = total + jnp.dot(four_terms(strips[0, k]), right, preferred_element_type=F32)
    image[...] = total[:block] + total[block:]


def group_specs(basis_rows, tile, g0, groups):
    specs, arrays = [], []
    for g in range(g0, g0 + groups):
        for part in (0, 1):
            for two in basis_rows:
                for m in range(two[part].shape[0]):
                    specs.append(pl.BlockSpec((1, tile, GROUP), lambda i, m=m, g=g: (m, i, g)))
                    arrays.append(two[part])
    return specs, arrays


def wide_parts(basis, orders, g):
    at = 2 * orders * g
    return [
        jnp.concatenate([x[0] for x in basis[at + p * orders:at + (p + 1) * orders]], 1)
        for p in (0, 1)]


def apply(places, ends, strips, pieces):
    row_blocks, near, block, _ = strips.shape
    rows, width = pieces[0][0].shape
    counts = [len(p) for p in pieces]
    flat = [x for p in pieces for x in p]
    return pl.pallas_call(
        functools.partial(apply_kernel, counts, near),
        grid=(row_blocks,),
        out_shape=jax.ShapeDtypeStruct((rows, width), F32),
        in_specs=[SMEM, SMEM, pl.BlockSpec((1, near, block, block), lambda i: (i, 0, 0, 0))]
        + [ANY] * len(flat),
        out_specs=pl.BlockSpec((block, width), lambda i: (i, 0)),
        scratch_shapes=[
            pltpu.VMEM((len(counts), rows, width), F32),
            pltpu.VMEM((len(counts) * rows * 2 + 2 * block, width), BF16),
            pltpu.SemaphoreType.DMA((len(counts),)),
        ],
        compiler_params=params(),
        cost_estimate=pl.CostEstimate(
            flops=8 * row_blocks * near * block * block * width,
            bytes_accessed=strips.size * 4 + 8 * rows * width * 4, transcendentals=0),
        name="apply",
    )(places, ends, strips, *flat)


def apply_late_kernel(counts, chosen, found, number, ends, begun, strips, *rest):
    pieces = rest[:sum(counts)]
    image, raw, window, held, total, sems, strip_sems = rest[sum(counts):]
    row_blocks, room, block, _ = held.shape
    rows, width = raw.shape[1], raw.shape[2]

    def copy(i, j):
        return pltpu.make_async_copy(strips.at[i, chosen[i, j]], held.at[i, j], strip_sems.at[i, j])

    def each(i, do):
        for j0 in range(0, room, TOGETHER):
            @pl.when(j0 < number[i])
            def _(j0=j0):
                do(range(j0, j0 + TOGETHER))

    def start(i, carry):
        def do(js):
            for j in js:
                copy(i, j).start()

        each(i, do)
        return carry

    lax.fori_loop(0, row_blocks, start, 0)
    load_window(pieces, counts, ends, raw, window, sems, block)
    window[len(counts) * rows * 2:, :] = jnp.zeros((2 * block, width), BF16)

    def one(i, carry):
        total[:block] = begun[aligned(i, block), :]
        total[block:] = jnp.zeros((block, width), F32)

        def do(js):
            for j in js:
                copy(i, j).wait()
            left = jnp.concatenate([four_terms(held[i, j]) for j in js], 1)
            right = jnp.concatenate(
                [window[aligned(found[i, j], 2 * block), :] for j in js], 0)
            total[...] += jnp.dot(left, right, preferred_element_type=F32)

        each(i, do)
        image[aligned(i, block), :] = total[:block] + total[block:]
        return carry

    lax.fori_loop(0, row_blocks, one, 0)


def apply_late(listed, ends, strips, pieces, begun):
    row_blocks, _, block, _ = strips.shape
    rows, width = begun.shape
    room = listed[0].shape[1]
    counts = [len(p) for p in pieces]
    flat = [x for p in pieces for x in p]
    return pl.pallas_call(
        functools.partial(apply_late_kernel, counts),
        out_shape=jax.ShapeDtypeStruct((rows, width), F32),
        in_specs=[SMEM] * 4 + [VMEM] + [ANY] * (1 + len(flat)),
        out_specs=VMEM,
        scratch_shapes=[
            pltpu.VMEM((len(counts), rows, width), F32),
            pltpu.VMEM((len(counts) * rows * 2 + 2 * block, width), BF16),
            pltpu.VMEM((row_blocks, room, block, block), F32),
            pltpu.VMEM((2 * block, width), F32),
            pltpu.SemaphoreType.DMA((len(counts),)),
            pltpu.SemaphoreType.DMA((row_blocks, room)),
        ],
        compiler_params=params(),
        cost_estimate=pl.CostEstimate(
            flops=4 * row_blocks * room * block * block * width,
            bytes_accessed=8 * rows * width * 4, transcendentals=0),
        name="apply_late",
    )(*listed, ends, begun, strips, *flat)


def list_late(place, inside, early, count, local_blocks):
    near = place.shape[1]
    most = min(near, (count - early) * local_blocks)
    room = -(-most // TOGETHER) * TOGETHER
    late = place >= early
    number = jnp.sum(late, axis=1, dtype=jnp.int32)
    rank = jnp.cumsum(late, axis=1, dtype=jnp.int32) - 1
    slots = jnp.arange(room)
    picked = (late & (slots[:, None, None] == rank)).astype(jnp.int32)
    chosen = jnp.sum(picked * jnp.arange(near), axis=2, dtype=jnp.int32).T
    found = jnp.sum(picked * ((place - early) * local_blocks + inside), axis=2, dtype=jnp.int32).T
    found = jnp.where(slots < number[:, None], found, (count - early) * local_blocks)
    return chosen, found, number


def inner_kernel(orders, image, *rest):
    basis, partial = rest[:-1], rest[-1]

    @pl.when(pl.program_id(0) == 0)
    def _():
        partial[...] = jnp.zeros_like(partial)

    for g in range(partial.shape[0]):
        cols = slice(g * GROUP, (g + 1) * GROUP)
        partial[g] += dot3_parts(
            split(image[:, cols]), wide_parts(basis, orders, g), ((0,), (0,)))


def inner(image, at, basis_rows, g0, groups):
    rows, width = image.shape[0], groups * GROUP
    orders = sum(two[0].shape[0] for two in basis_rows)
    tile = rows // 4
    specs, arrays = group_specs(basis_rows, tile, g0, groups)
    shape = (groups, GROUP, orders * GROUP)
    return pl.pallas_call(
        functools.partial(inner_kernel, orders),
        grid=(rows // tile,),
        out_shape=jax.ShapeDtypeStruct(shape, F32),
        in_specs=[pl.BlockSpec((tile, width), lambda i: (i, at // groups))] + specs,
        out_specs=pl.BlockSpec(shape, lambda i: (0, 0, 0)),
        compiler_params=params(),
        cost_estimate=pl.CostEstimate(
            flops=24 * rows * width * GROUP, bytes_accessed=5 * rows * width * 4,
            transcendentals=0),
        name="inner",
    )(image, *arrays)


def project_kernel(orders, image, coeffs_t, *rest):
    groups = coeffs_t.shape[0]
    basis, (residual, gram) = rest[:-2], rest[-2:]

    @pl.when(pl.program_id(0) == 0)
    def _():
        gram[...] = jnp.zeros_like(gram)

    for g in range(groups):
        cols = slice(g * GROUP, (g + 1) * GROUP)
        left = image[:, cols] - dot3_parts(
            wide_parts(basis, orders, g), split(coeffs_t[g]), ((1,), (1,)))
        residual[:, cols] = left
        parts = split(left)
        gram[g] += dot3_parts(parts, parts, ((0,), (0,)))


def project(image, at, basis_rows, coeffs_t, g0, groups):
    orders = sum(two[0].shape[0] for two in basis_rows)
    rows, width = image.shape[0], groups * GROUP
    tile = rows // 4
    specs, arrays = group_specs(basis_rows, tile, g0, groups)
    return pl.pallas_call(
        functools.partial(project_kernel, orders),
        grid=(rows // tile,),
        out_shape=[
            jax.ShapeDtypeStruct((rows, width), F32),
            jax.ShapeDtypeStruct((groups, GROUP, GROUP), F32),
        ],
        in_specs=[
            pl.BlockSpec((tile, width), lambda i: (i, at // groups)),
            pl.BlockSpec(coeffs_t.shape, lambda i: (0, 0, 0)),
        ] + specs,
        out_specs=[
            pl.BlockSpec((tile, width), lambda i: (i, 0)),
            pl.BlockSpec((groups, GROUP, GROUP), lambda i: (0, 0, 0)),
        ],
        compiler_params=params(),
        cost_estimate=pl.CostEstimate(
            flops=30 * rows * width * GROUP, bytes_accessed=6 * rows * width * 4,
            transcendentals=0),
        name="project",
    )(image, coeffs_t, *arrays)


def eliminate(gram):
    count = len(gram)
    order = gram[0].shape[0]
    row_at = lax.broadcasted_iota(jnp.int32, (order, order), 0)
    col_at = lax.broadcasted_iota(jnp.int32, (order, order), 1)
    eye = jnp.where(row_at == col_at, 1.0, 0.0).astype(F32)
    rest = [jnp.concatenate([g, eye], 1) for g in gram]
    done = [[] for _ in gram]
    panel_row = lax.broadcasted_iota(jnp.int32, (PANEL, order), 0)
    for p0 in range(0, order, PANEL):
        panels = [r[:PANEL] for r in rest]
        inverse_pivots = [[] for _ in gram]
        for j0 in range(0, PANEL, AHEAD):
            ahead = [
                [jnp.broadcast_to(panel[:, p0 + j:p0 + j + 1], (PANEL, order))
                 for j in range(j0, j0 + AHEAD)] for panel in panels]
            for t in range(AHEAD):
                j = j0 + t
                for n in range(count):
                    columns, panel = ahead[n], panels[n]
                    inverse = 1.0 / columns[t][j:j + 1]
                    factor = jnp.where(panel_row > j, columns[t] * inverse, 0.0)
                    for u in range(t + 1, AHEAD):
                        columns[u] = columns[u] - factor * columns[u][j:j + 1]
                    panels[n] = panel - jnp.concatenate([factor, factor], 1) * panel[j:j + 1]
                    inverse_pivots[n].append(inverse)
        for n in range(count):
            scale = jnp.sqrt(jnp.concatenate(inverse_pivots[n], 0))
            panel = panels[n] * jnp.concatenate([scale, scale], 1)
            done[n].append(panel)
            if p0 + PANEL < order:
                below = panel[:, p0 + PANEL:order]
                rest[n] = rest[n][PANEL:] - lax.dot_general(
                    below, panel, (((0,), (0,)), ((), ())),
                    precision=lax.Precision.HIGHEST, preferred_element_type=F32)
    lowers, inverses = [], []
    for n in range(count):
        upper = jnp.concatenate(done[n], 0)
        lowers.append(jnp.where(row_at >= col_at, upper[:, :order].T, 0.0))
        inverses.append(upper[:, order:])
    return lowers, inverses


def with_factor(k):
    return k < 2 or not k & 1


def finish_kernel(groups, parts, me, gram, residual, *outs):
    lowers, inverses = eliminate([gram[g] for g in range(groups)])
    rows = residual.shape[0] // parts
    for k in range(parts):
        for g in range(groups):
            cols = slice(g * GROUP, (g + 1) * GROUP)
            left = residual[aligned(me[0] ^ k, rows), cols]
            outs[k][:rows, cols] = dot3(left, inverses[g], ((1,), (1,)))
            if with_factor(k):
                outs[k][rows:, cols] = lowers[g]


def finish(me, gram, residual, parts):
    groups = gram.shape[0]
    rows, width = residual.shape
    shapes = [
        jax.ShapeDtypeStruct((rows // parts + GROUP * with_factor(k), width), F32)
        for k in range(parts)]
    return pl.pallas_call(
        functools.partial(finish_kernel, groups, parts),
        out_shape=shapes,
        in_specs=[SMEM, VMEM, VMEM],
        out_specs=[VMEM] * parts,
        compiler_params=params(),
        cost_estimate=pl.CostEstimate(
            flops=6 * rows * width * GROUP, bytes_accessed=4 * rows * width * 4,
            transcendentals=0),
        name="finish",
    )(me, gram, residual)


def collect_blocks(me, blocks, factors, chunks, new_shape, factor_shape, parts):
    rows = new_shape[0]
    step = new_shape[1] // parts
    per_part = step // GROUP
    alone = [(c, k) for c in range(len(chunks)) for k in range(parts) if not with_factor(k)]

    def kernel(me_ref, *refs):
        new_out, factor_out = refs[-2:]
        for c, (g0, groups) in enumerate(chunks):
            for k in range(parts):
                src = refs[c * parts + k]
                at = me_ref[0] ^ k
                if (c, k) in alone:
                    factor = refs[len(chunks) * parts + alone.index((c, k))]
                else:
                    factor = src.at[pl.ds(rows, GROUP), :]
                for g in range(groups):
                    cols = slice(g * GROUP, (g + 1) * GROUP)
                    group = at * per_part + g0 + g
                    new_out[:, aligned(group, GROUP)] = src[:rows, cols]
                    factor_out[group] = factor[:, cols]

    return pl.pallas_call(
        kernel,
        out_shape=[jax.ShapeDtypeStruct(new_shape, F32), jax.ShapeDtypeStruct(factor_shape, F32)],
        in_specs=[SMEM] + [VMEM] * (len(chunks) * parts + len(alone)),
        out_specs=[VMEM] * 2,
        compiler_params=params(),
        name="collect_blocks",
    )(me, *[x for c in blocks for x in c], *[factors[c][k] for c, k in alone])


def collect_coeffs(me, coeffs, chunks, shape, parts):
    per_part = shape[1] // parts

    def kernel(me_ref, *refs):
        for c, (g0, groups) in enumerate(chunks):
            for k in range(parts):
                for g in range(groups):
                    for m in range(shape[0]):
                        refs[-1][m, (me_ref[0] ^ k) * per_part + g0 + g] = (
                            refs[c * parts + k][g, :, m * GROUP:(m + 1) * GROUP].T)

    return pl.pallas_call(
        kernel,
        out_shape=jax.ShapeDtypeStruct(shape, F32),
        in_specs=[SMEM] + [VMEM] * (len(chunks) * parts),
        out_specs=VMEM,
        compiler_params=params(),
        name="collect_coeffs",
    )(me, *[x for c in coeffs for x in c])


class Sum:
    def __init__(self, value):
        self.shape = value.shape
        self.value = value.reshape(-1, value.shape[-1])
        self.side = lax.axis_index("blk") % 2
        whole = [k for k in (1 << i for i in range(16)) if k < lax.axis_size("blk")]
        long = self.value.shape[0] > HALVED and len(whole) > 1
        self.steps = ["halve", *whole[1:], "join"] if long else whole

    def step(self):
        kind = self.steps.pop(0)
        if kind == "halve":
            half = self.value.shape[0] // 2
            kept = lax.dynamic_slice_in_dim(self.value, self.side * half, half, 0)
            sent = lax.dynamic_slice_in_dim(self.value, (1 - self.side) * half, half, 0)
            self.value = kept + swap(sent, "blk", 1)
        elif kind == "join":
            other = swap(self.value, "blk", 1)
            first = self.side == 0
            self.value = jnp.concatenate(
                [jnp.where(first, self.value, other), jnp.where(first, other, self.value)], 0)
        else:
            self.value = self.value + swap(self.value, "blk", kind)

    def result(self):
        while self.steps:
            self.step()
        return self.value.reshape(self.shape)


def local(strips, near_cols, vector_block, basis):
    local_blocks = strips.shape[0]
    devices = lax.axis_size("blk")
    parts = lax.axis_size("rhs")
    hops = -(-BAND // local_blocks)
    rows, total = vector_block.shape
    step = total // parts
    groups = step // GROUP
    orders = basis.shape[0]
    chunks = [(0, groups - groups // 2), (groups - groups // 2, groups // 2)]
    chunks = [chunk for chunk in chunks if chunk[1]]
    me = lax.axis_index("rhs").astype(jnp.int32).reshape(1)
    blk = lax.axis_index("blk")
    others = list(range(1, parts))
    relayed = two_lines(devices, hops) and len(chunks) == 2

    table = plan_window(devices, hops)
    place = jnp.asarray(table)[blk][near_cols // local_blocks]
    inside = near_cols % local_blocks
    places = place * local_blocks + inside
    count = int(table.max()) + 1
    early = count - 2
    early_places = jnp.where(place < early, places, early * local_blocks)
    listed = list_late(place, inside, early, count, local_blocks)
    ends = jnp.where((blk < 2) | (blk >= devices - 2), 1, 0).astype(jnp.int32).reshape(1)

    vector = vector_block[None]
    half = -(-orders // 2)
    values = {}

    def send(key):
        kind, at, k = key
        values[key] = swap(values["cut", kind, at, k], "rhs", k)

    def cut(kind, at, value, layer, layers, c0, width):
        for k, x in zip(others, cut_columns(
                value, layer, layers, me, others, c0, width, parts)):
            values["cut", kind, at, k] = x

    def join(kind, at, value, layer, layers, c0, width):
        got = [values[kind, at, k] for k in others]
        return join_rows(value, layer, layers, got, me, c0, width, parts, kind == "b")

    def own_rows(c):
        c0, width = chunks[c][0] * GROUP, chunks[c][1] * GROUP
        values["own", c] = join("v", c, vector, 0, 1, c0, width)[0][0]

    for c, (g0, n) in enumerate(chunks):
        cut("v", c, vector, 0, 1, g0 * GROUP, n * GROUP)
    layers = [(m, min(half, orders - m)) for m in range(0, orders, half)]
    for h, (m, n) in enumerate(layers):
        cut("b", h, basis, m, n, 0, step)

    def barrier(flying=()):
        keys = [key for key in values if key not in flying]
        for key, x in zip(keys, lax.optimization_barrier(tuple(values[k] for k in keys))):
            values[key] = x

    def window(c, names=PLACES):
        return [[values[n, c] for n in alternatives] for alternatives in names]

    for k in others:
        send(("v", 0, k))
    own_rows(0)
    if relayed:
        plan = relay_plan()
        beside = {h: [("b", h, 1)] for h in range(len(layers))}
        for i, (h, k) in enumerate((h, k) for h in range(len(layers)) for k in others if k > 1):
            beside.setdefault(i, []).append(("b", h, k))
        def join_basis(h):
            values["high", h], values["low", h] = join("b", h, basis, *layers[h], 0, step)

        def basis_parts():
            return [(values["high", h], values["low", h]) for h in range(len(layers))]

        def early_part(c):
            values["begun", c] = apply(early_places, ends, strips, window(c, PLACES[:early]))

        def late_part(c):
            return apply_late(
                listed, ends, strips, window(c, PLACES[early:]), values.pop(("begun", c)))

        def early_part(c):
            values["begun", c] = apply(early_places, ends, strips, window(c, PLACES[:early]))

        def late_part(c):
            values["image", c] = apply_late(
                listed, ends, strips, window(c, PLACES[early:]), values.pop(("begun", c)))

        def relay(name, c):
            source, pairs = plan[name]
            if isinstance(source, tuple):
                value = jnp.where(ends[0] == 0, *[values[x, c] for x in source])
            else:
                value = values[source, c]
            values[name, c] = lax.ppermute(value, "blk", pairs)

        def add_step(running):
            running.value = values["sum"]
            running.step()
            values["sum"] = running.value

        for r, relays in enumerate(ROUNDS):
            flying = list(beside.get(r, ()))
            for name, c in relays:
                relay(name, c)
            if r == 0:
                for k in others:
                    send(("v", 1, k))
                own_rows(1)
            for key in flying:
                send(key)
            if r == 3:
                join_basis(0)
            if r == 4:
                for h in range(1, len(layers)):
                    join_basis(h)
                values["image", 0] = apply(places, ends, strips, window(0))
                values["sum"] = inner(values["image", 0], 0, basis_parts(), *chunks[0])
            if r == 5:
                first = Sum(values["sum"])
                first.step()
                values["sum"] = first.value
                early_part(1)
            barrier(flying)
        basis_rows = basis_parts()
    else:
        for c in range(1, len(chunks)):
            for k in others:
                send(("v", c, k))
            own_rows(c)
        for h in range(len(layers)):
            for k in others:
                send(("b", h, k))
        basis_rows = [join("b", h, basis, m, n, 0, step) for h, (m, n) in enumerate(layers)]
        for c in range(len(chunks)):
            pieces = []
            for offset in window_offsets(devices, hops):
                pairs = [((i + offset) % devices, i) for i in range(devices)]
                own = values["own", c]
                pieces.append([lax.ppermute(own, "blk", pairs) if offset else own])
            values["image", c] = apply(places, ends, strips, pieces)

    def spread(value):
        got = [value]
        for k in (1 << i for i in range(16)):
            if 1 < k < parts:
                got += [swap(x, "rhs", k) for x in got]
        pair = [swap(x, "rhs", 1) for x in got]
        return [x for two in zip(got, pair) for x in two]

    def tied(*xs):
        return lax.optimization_barrier(tuple(xs))

    def tie(*running):
        for one, x in zip(running, tied(*[one.value for one in running])):
            one.value = x

    def projected(c, coeffs_t):
        g0, n = chunks[c]
        all_coeffs.append(spread(coeffs_t))
        residual, gram = project(values["image", c], 0, basis_rows, coeffs_t, g0, n)
        residuals.append(residual)
        return Sum(gram)

    all_coeffs, residuals, blocks = [], [], []
    last = len(chunks) - 1
    if relayed:
        first.value = values["sum"]
        first.step()
        late_part(1)
        first.value, values["image", 1] = tied(first.value, values["image", 1])
        first.step()
        second = Sum(inner(values["image", 1], 0, basis_rows, *chunks[1]))
        second.step()
        second.step()
        first.step()
        tie(first, second)
        second.step()
        grams = [projected(0, first.result())]
        tie(second, grams[0])
        second.step()
        grams[0].step()
        tie(second, grams[0])
        grams.append(projected(1, second.result()))
        grams[0].step()
        tie(*grams)
    else:
        grams = [
            projected(c, Sum(inner(values["image", c], 0, basis_rows, *chunks[c])).result())
            for c in range(len(chunks))]
    grams = [gram.result() for gram in grams]
    held = [x for got in all_coeffs for x in got]
    grams[-1], *held = tied(grams[-1], *held)
    all_coeffs = [held[c * parts:(c + 1) * parts] for c in range(len(chunks))]
    for residual, gram in zip(residuals, grams):
        out = finish(me, gram, residual, parts)
        got = [out[0]] + [swap(out[k], "rhs", k) for k in others]
        blocks.append(got)

    coeffs = collect_coeffs(
        me, all_coeffs, chunks, (orders, total // GROUP, GROUP, GROUP), parts)
    factors = []
    for c, got in enumerate(blocks):
        far = {k: got[k ^ 1][rows:] for k in others if not with_factor(k)}
        if c == last and far:
            k = max(far)
            far[k], coeffs = tied(far[k], coeffs)
        factors.append({k: swap(x, "rhs", 1) for k, x in far.items()})
    new_block, factor = collect_blocks(
        me, blocks, factors, chunks, (rows, total), (total // GROUP, GROUP, GROUP), parts)
    return new_block, coeffs, factor


def solution(mesh):
    placed = (
        P("blk", None, None, None),
        P("blk", None),
        P(("blk", "rhs"), None),
        P(None, ("blk", "rhs"), None),
    )
    return jax.shard_map(
        local,
        mesh=mesh,
        in_specs=placed,
        out_specs=(P(("blk", "rhs"), None), P(), P()),
        check_vma=False,
    )
```

```python
import functools

import jax
import jax.numpy as jnp
import numpy as np
from jax import lax
from jax.experimental import pallas as pl
from jax.experimental.pallas import tpu as pltpu
from jax.sharding import PartitionSpec as P

GROUP = 128
BAND = 24
PANEL = 32
AHEAD = 8
TOGETHER = 8
HALVED = 128

F32 = jnp.float32
BF16 = jnp.bfloat16
ANY = pl.BlockSpec(memory_space=pl.ANY)
SMEM = pl.BlockSpec(memory_space=pltpu.SMEM)
VMEM = pl.BlockSpec(memory_space=pltpu.VMEM)
LIMIT = 50 * 1024 * 1024


def params(**kw):
    return pltpu.CompilerParams(vmem_limit_bytes=LIMIT, **kw)


def pairs_of(axis, k):
    return [(i, i ^ k) for i in range(lax.axis_size(axis))]


def swap(value, axis, k):
    return lax.ppermute(value, axis, pairs_of(axis, k))


def split(value):
    high = value.astype(BF16)
    return high, (value - high.astype(F32)).astype(BF16)


def dot3(a, b, dims):
    return dot3_parts(split(a), split(b), dims)


def dot3_parts(a, b, dims):
    (a_high, a_low), (b_high, b_low) = a, b

    def one(x, y):
        return lax.dot_general(x, y, (dims, ((), ())), preferred_element_type=F32)

    return one(a_high, b_high) + (one(a_high, b_low) + one(a_low, b_high))


def aligned(index, step):
    return pl.ds(pl.multiple_of(index * step, step), step)


def column_spec(value, layer, parts, k):
    rows, step = value.shape[1], value.shape[2] // parts
    return pl.BlockSpec((1, rows, step), lambda i, me: (layer + i, 0, me[0] ^ k))


def layer_spec(rows, width):
    return pl.BlockSpec((1, rows, width), lambda i, me: (i, 0, 0))


def cut_columns(value, layer, layers, me, ks, c0, width, parts, after=()):
    rows = value.shape[1]

    def kernel(me_ref, *refs):
        for src, dst in zip(refs, refs[-len(ks):]):
            dst[...] = src[:, :, c0:c0 + width]

    return pl.pallas_call(
        kernel,
        grid_spec=pltpu.PrefetchScalarGridSpec(
            num_scalar_prefetch=1,
            grid=(layers,),
            in_specs=[column_spec(value, layer, parts, k) for k in ks] + [ANY] * len(after),
            out_specs=[layer_spec(rows, width)] * len(ks),
        ),
        out_shape=[jax.ShapeDtypeStruct((layers, rows, width), value.dtype)] * len(ks),
        compiler_params=params(),
        name="cut_columns",
    )(me, *[value] * len(ks), *after)


def join_rows(value, layer, layers, received, me, c0, width, parts, halves=False):
    rows = value.shape[1]
    types = [BF16, BF16] if halves else [value.dtype]

    def kernel(me_ref, *refs):
        for k in range(parts):
            at = c0 if k == 0 else 0
            piece = refs[k][0, :, at:at + width]
            for out, x in zip(refs[parts:], split(piece) if halves else [piece]):
                out[0, aligned(me_ref[0] ^ k, rows), :] = x

    return pl.pallas_call(
        kernel,
        grid_spec=pltpu.PrefetchScalarGridSpec(
            num_scalar_prefetch=1,
            grid=(layers,),
            in_specs=[column_spec(value, layer, parts, 0)]
            + [layer_spec(rows, width)] * (parts - 1),
            out_specs=[layer_spec(rows * parts, width)] * len(types),
        ),
        out_shape=[jax.ShapeDtypeStruct((layers, rows * parts, width), t) for t in types],
        compiler_params=params(),
        name="join_rows",
    )(me, value, *received)


def two_lines(devices, hops):
    return devices == 8 and devices == 2 * hops + 2


def window_offsets(devices, hops):
    seen = []
    for offset in range(-hops, hops + 1):
        if offset % devices not in seen:
            seen.append(offset % devices)
    return sorted(seen, key=lambda offset: min(offset, devices - offset))


def plan_window(devices, hops):
    table = np.zeros((devices, devices), np.int32)
    if two_lines(devices, hops):
        for z in range(4):
            for y in range(2):
                inner, far, back = z in (1, 2), 3 - z, 1 - y
                places = [
                    (z, y), (z ^ 1, y), (z, back), (z ^ 1, back), (far, back if inner else y),
                    (far, y) if inner else (2 if z == 0 else 1, back),
                    (3 if z == 1 else 0, back) if inner else (far, back),
                ]
                for place, (a, b) in enumerate(places):
                    table[2 * z + y, 2 * a + b] = place
        return table
    for d in range(devices):
        for place, offset in enumerate(window_offsets(devices, hops)):
            table[d, (d + offset) % devices] = place
    return table


def relay_plan():
    def lines(pairs):
        return [(2 * a + y, 2 * b + y) for a, b in pairs for y in (0, 1)]

    outer = lines([(0, 1), (1, 0), (2, 3), (3, 2)])
    middle = lines([(1, 2), (2, 1)])
    to_ends = lines([(1, 0), (2, 3)])
    across = [(i, i ^ 1) for i in range(8)]
    return {
        "q1": ("own", outer), "y1": ("own", across), "q2": ("own", middle),
        "q3": ("q1", middle), "y2": ("q1", across), "q5": ("y1", middle),
        "q4": ("q3", to_ends), "q6": ("q5", to_ends),
        "y3": (("q3", "q4"), across),
    }


ROUNDS = (
    (("q1", 0), ("y1", 0), ("q2", 0)),
    (("q3", 0), ("y2", 0), ("q1", 1)),
    (("q5", 0), ("q4", 0), ("y1", 1)),
    (("q6", 0), ("y3", 0), ("q3", 1)),
    (("q5", 1), ("q4", 1), ("y2", 1)),
    (("q6", 1), ("y3", 1), ("q2", 1)),
)
PLACES = (("own",), ("q1",), ("y1",), ("y2",), ("q5", "q4"), ("q2", "q6"), ("y3",))


def load_window(pieces, counts, ends, raw, window, sems, block):
    rows = raw.shape[1]
    at = 0
    for place, count in enumerate(counts):
        for end in range(count):
            def fetch(at=at, place=place, end=end):
                pltpu.make_async_copy(pieces[at + end], raw.at[place], sems.at[place]).start()

            if count == 1:
                fetch()
            else:
                pl.when(ends[0] == end)(fetch)
        at += count
    for place in range(len(counts)):
        pltpu.make_async_copy(pieces[0], raw.at[place], sems.at[place]).wait()

        def one(i, carry, place=place):
            high, low = split(raw[place, aligned(i, block), :])
            base = (place * (rows // block) + i) * 2
            window[aligned(base, block), :] = high
            window[aligned(base + 1, block), :] = low
            return carry

        lax.fori_loop(0, rows // block, one, 0)


def four_terms(strip):
    high, low = split(strip)
    return jnp.concatenate(
        [jnp.concatenate([high, high], 1), jnp.concatenate([low, low], 1)], 0)


def apply_kernel(counts, near, places, ends, strips, *rest):
    pieces = rest[:sum(counts)]
    image, raw, window, sems = rest[sum(counts):]
    step = pl.program_id(0)
    block = strips.shape[2]

    @pl.when(step == 0)
    def _():
        load_window(pieces, counts, ends, raw, window, sems, block)
        window[len(counts) * raw.shape[1] * 2:, :] = jnp.zeros((2 * block, raw.shape[2]), BF16)

    total = jnp.zeros((2 * block, raw.shape[2]), F32)
    for k in range(near):
        right = window[aligned(places[step, k], 2 * block), :]
        total = total + jnp.dot(four_terms(strips[0, k]), right, preferred_element_type=F32)
    image[...] = total[:block] + total[block:]


def group_specs(basis_rows, tile, g0, groups):
    specs, arrays = [], []
    for g in range(g0, g0 + groups):
        for part in (0, 1):
            for two in basis_rows:
                for m in range(two[part].shape[0]):
                    specs.append(pl.BlockSpec((1, tile, GROUP), lambda i, m=m, g=g: (m, i, g)))
                    arrays.append(two[part])
    return specs, arrays


def wide_parts(basis, orders, g):
    at = 2 * orders * g
    return [
        jnp.concatenate([x[0] for x in basis[at + p * orders:at + (p + 1) * orders]], 1)
        for p in (0, 1)]


def apply(places, ends, strips, pieces):
    row_blocks, near, block, _ = strips.shape
    rows, width = pieces[0][0].shape
    counts = [len(p) for p in pieces]
    flat = [x for p in pieces for x in p]
    return pl.pallas_call(
        functools.partial(apply_kernel, counts, near),
        grid=(row_blocks,),
        out_shape=jax.ShapeDtypeStruct((rows, width), F32),
        in_specs=[SMEM, SMEM, pl.BlockSpec((1, near, block, block), lambda i: (i, 0, 0, 0))]
        + [ANY] * len(flat),
        out_specs=pl.BlockSpec((block, width), lambda i: (i, 0)),
        scratch_shapes=[
            pltpu.VMEM((len(counts), rows, width), F32),
            pltpu.VMEM((len(counts) * rows * 2 + 2 * block, width), BF16),
            pltpu.SemaphoreType.DMA((len(counts),)),
        ],
        compiler_params=params(),
        cost_estimate=pl.CostEstimate(
            flops=8 * row_blocks * near * block * block * width,
            bytes_accessed=strips.size * 4 + 8 * rows * width * 4, transcendentals=0),
        name="apply",
    )(places, ends, strips, *flat)


def apply_late_kernel(counts, chosen, found, number, ends, begun, strips, *rest):
    pieces = rest[:sum(counts)]
    image, raw, window, held, total, before, sems, strip_sems = rest[sum(counts):]
    row_blocks, room, block, _ = held.shape
    rows, width = raw.shape[1], raw.shape[2]

    def copy(i, j):
        return pltpu.make_async_copy(strips.at[i, chosen[i, j]], held.at[i, j], strip_sems.at[i, j])

    def each(i, do):
        for j0 in range(0, room, TOGETHER):
            @pl.when(j0 < number[i])
            def _(j0=j0):
                do(range(j0, j0 + TOGETHER))

    def start(i, carry):
        def do(js):
            for j in js:
                copy(i, j).start()

        each(i, do)
        return carry

    bring = pltpu.make_async_copy(begun, before, sems.at[len(counts)])
    bring.start()
    lax.fori_loop(0, row_blocks, start, 0)
    load_window(pieces, counts, ends, raw, window, sems, block)
    window[len(counts) * rows * 2:, :] = jnp.zeros((2 * block, width), BF16)

    bring.wait()

    def one(i, carry):
        total[:block] = before[aligned(i, block), :]
        total[block:] = jnp.zeros((block, width), F32)

        def do(js):
            for j in js:
                copy(i, j).wait()
            left = jnp.concatenate([four_terms(held[i, j]) for j in js], 1)
            right = jnp.concatenate(
                [window[aligned(found[i, j], 2 * block), :] for j in js], 0)
            total[...] += jnp.dot(left, right, preferred_element_type=F32)

        each(i, do)
        image[aligned(i, block), :] = total[:block] + total[block:]
        return carry

    lax.fori_loop(0, row_blocks, one, 0)


def apply_late(listed, ends, strips, pieces, begun):
    row_blocks, _, block, _ = strips.shape
    rows, width = begun.shape
    room = listed[0].shape[1]
    counts = [len(p) for p in pieces]
    flat = [x for p in pieces for x in p]
    return pl.pallas_call(
        functools.partial(apply_late_kernel, counts),
        out_shape=jax.ShapeDtypeStruct((rows, width), F32),
        in_specs=[SMEM] * 4 + [ANY] * (2 + len(flat)),
        out_specs=VMEM,
        scratch_shapes=[
            pltpu.VMEM((len(counts), rows, width), F32),
            pltpu.VMEM((len(counts) * rows * 2 + 2 * block, width), BF16),
            pltpu.VMEM((row_blocks, room, block, block), F32),
            pltpu.VMEM((2 * block, width), F32),
            pltpu.VMEM((rows, width), F32),
            pltpu.SemaphoreType.DMA((len(counts) + 1,)),
            pltpu.SemaphoreType.DMA((row_blocks, room)),
        ],
        compiler_params=params(),
        cost_estimate=pl.CostEstimate(
            flops=4 * row_blocks * room * block * block * width,
            bytes_accessed=8 * rows * width * 4, transcendentals=0),
        name="apply_late",
    )(*listed, ends, begun, strips, *flat)


def list_late(place, inside, early, count, local_blocks):
    near = place.shape[1]
    most = min(near, (count - early) * local_blocks)
    room = -(-most // TOGETHER) * TOGETHER
    late = place >= early
    number = jnp.sum(late, axis=1, dtype=jnp.int32)
    rank = jnp.cumsum(late, axis=1, dtype=jnp.int32) - 1
    slots = jnp.arange(room)
    picked = (late & (slots[:, None, None] == rank)).astype(jnp.int32)
    chosen = jnp.sum(picked * jnp.arange(near), axis=2, dtype=jnp.int32).T
    found = jnp.sum(picked * ((place - early) * local_blocks + inside), axis=2, dtype=jnp.int32).T
    found = jnp.where(slots < number[:, None], found, (count - early) * local_blocks)
    return chosen, found, number


def inner_kernel(orders, image, *rest):
    basis, partial = rest[:-1], rest[-1]

    @pl.when(pl.program_id(0) == 0)
    def _():
        partial[...] = jnp.zeros_like(partial)

    for g in range(partial.shape[0]):
        cols = slice(g * GROUP, (g + 1) * GROUP)
        partial[g] += dot3_parts(
            split(image[:, cols]), wide_parts(basis, orders, g), ((0,), (0,)))


def inner(image, at, basis_rows, g0, groups):
    rows, width = image.shape[0], groups * GROUP
    orders = sum(two[0].shape[0] for two in basis_rows)
    tile = rows // 2
    specs, arrays = group_specs(basis_rows, tile, g0, groups)
    shape = (groups, GROUP, orders * GROUP)
    return pl.pallas_call(
        functools.partial(inner_kernel, orders),
        grid=(rows // tile,),
        out_shape=jax.ShapeDtypeStruct(shape, F32),
        in_specs=[pl.BlockSpec((tile, width), lambda i: (i, at // groups))] + specs,
        out_specs=pl.BlockSpec(shape, lambda i: (0, 0, 0)),
        compiler_params=params(),
        cost_estimate=pl.CostEstimate(
            flops=24 * rows * width * GROUP, bytes_accessed=5 * rows * width * 4,
            transcendentals=0),
        name="inner",
    )(image, *arrays)


def project_kernel(orders, image, coeffs_t, *rest):
    groups = coeffs_t.shape[0]
    basis, (residual, gram) = rest[:-2], rest[-2:]

    @pl.when(pl.program_id(0) == 0)
    def _():
        gram[...] = jnp.zeros_like(gram)

    for g in range(groups):
        cols = slice(g * GROUP, (g + 1) * GROUP)
        left = image[:, cols] - dot3_parts(
            wide_parts(basis, orders, g), split(coeffs_t[g]), ((1,), (1,)))
        residual[:, cols] = left
        parts = split(left)
        gram[g] += dot3_parts(parts, parts, ((0,), (0,)))


def project(image, at, basis_rows, coeffs_t, g0, groups):
    orders = sum(two[0].shape[0] for two in basis_rows)
    rows, width = image.shape[0], groups * GROUP
    tile = rows // 2
    specs, arrays = group_specs(basis_rows, tile, g0, groups)
    return pl.pallas_call(
        functools.partial(project_kernel, orders),
        grid=(rows // tile,),
        out_shape=[
            jax.ShapeDtypeStruct((rows, width), F32),
            jax.ShapeDtypeStruct((groups, GROUP, GROUP), F32),
        ],
        in_specs=[
            pl.BlockSpec((tile, width), lambda i: (i, at // groups)),
            pl.BlockSpec(coeffs_t.shape, lambda i: (0, 0, 0)),
        ] + specs,
        out_specs=[
            pl.BlockSpec((tile, width), lambda i: (i, 0)),
            pl.BlockSpec((groups, GROUP, GROUP), lambda i: (0, 0, 0)),
        ],
        compiler_params=params(),
        cost_estimate=pl.CostEstimate(
            flops=30 * rows * width * GROUP, bytes_accessed=6 * rows * width * 4,
            transcendentals=0),
        name="project",
    )(image, coeffs_t, *arrays)


def eliminate(gram):
    count = len(gram)
    order = gram[0].shape[0]
    row_at = lax.broadcasted_iota(jnp.int32, (order, order), 0)
    col_at = lax.broadcasted_iota(jnp.int32, (order, order), 1)
    eye = jnp.where(row_at == col_at, 1.0, 0.0).astype(F32)
    rest = [jnp.concatenate([g, eye], 1) for g in gram]
    done = [[] for _ in gram]
    panel_row = lax.broadcasted_iota(jnp.int32, (PANEL, order), 0)
    for p0 in range(0, order, PANEL):
        panels = [r[:PANEL] for r in rest]
        inverse_pivots = [[] for _ in gram]
        for j0 in range(0, PANEL, AHEAD):
            ahead = [
                [jnp.broadcast_to(panel[:, p0 + j:p0 + j + 1], (PANEL, order))
                 for j in range(j0, j0 + AHEAD)] for panel in panels]
            for t in range(AHEAD):
                j = j0 + t
                for n in range(count):
                    columns, panel = ahead[n], panels[n]
                    inverse = 1.0 / columns[t][j:j + 1]
                    factor = jnp.where(panel_row > j, columns[t] * inverse, 0.0)
                    for u in range(t + 1, AHEAD):
                        columns[u] = columns[u] - factor * columns[u][j:j + 1]
                    panels[n] = panel - jnp.concatenate([factor, factor], 1) * panel[j:j + 1]
                    inverse_pivots[n].append(inverse)
        for n in range(count):
            scale = jnp.sqrt(jnp.concatenate(inverse_pivots[n], 0))
            panel = panels[n] * jnp.concatenate([scale, scale], 1)
            done[n].append(panel)
            if p0 + PANEL < order:
                below = panel[:, p0 + PANEL:order]
                rest[n] = rest[n][PANEL:] - lax.dot_general(
                    below, panel, (((0,), (0,)), ((), ())),
                    precision=lax.Precision.HIGHEST, preferred_element_type=F32)
    lowers, inverses = [], []
    for n in range(count):
        upper = jnp.concatenate(done[n], 0)
        lowers.append(jnp.where(row_at >= col_at, upper[:, :order].T, 0.0))
        inverses.append(upper[:, order:])
    return lowers, inverses


def with_factor(k):
    return k < 2 or not k & 1


def finish_kernel(groups, parts, me, gram, residual, *outs):
    lowers, inverses = eliminate([gram[g] for g in range(groups)])
    rows = residual.shape[0] // parts
    for k in range(parts):
        for g in range(groups):
            cols = slice(g * GROUP, (g + 1) * GROUP)
            left = residual[aligned(me[0] ^ k, rows), cols]
            outs[k][:rows, cols] = dot3(left, inverses[g], ((1,), (1,)))
            if with_factor(k):
                outs[k][rows:, cols] = lowers[g]


def finish(me, gram, residual, parts):
    groups = gram.shape[0]
    rows, width = residual.shape
    shapes = [
        jax.ShapeDtypeStruct((rows // parts + GROUP * with_factor(k), width), F32)
        for k in range(parts)]
    return pl.pallas_call(
        functools.partial(finish_kernel, groups, parts),
        out_shape=shapes,
        in_specs=[SMEM, VMEM, VMEM],
        out_specs=[VMEM] * parts,
        compiler_params=params(),
        cost_estimate=pl.CostEstimate(
            flops=6 * rows * width * GROUP, bytes_accessed=4 * rows * width * 4,
            transcendentals=0),
        name="finish",
    )(me, gram, residual)


def collect_blocks(me, blocks, factors, chunks, new_shape, factor_shape, parts):
    rows = new_shape[0]
    step = new_shape[1] // parts
    per_part = step // GROUP
    alone = [(c, k) for c in range(len(chunks)) for k in range(parts) if not with_factor(k)]

    def kernel(me_ref, *refs):
        new_out, factor_out = refs[-2:]
        for c, (g0, groups) in enumerate(chunks):
            for k in range(parts):
                src = refs[c * parts + k]
                at = me_ref[0] ^ k
                if (c, k) in alone:
                    factor = refs[len(chunks) * parts + alone.index((c, k))]
                else:
                    factor = src.at[pl.ds(rows, GROUP), :]
                for g in range(groups):
                    cols = slice(g * GROUP, (g + 1) * GROUP)
                    group = at * per_part + g0 + g
                    new_out[:, aligned(group, GROUP)] = src[:rows, cols]
                    factor_out[group] = factor[:, cols]

    return pl.pallas_call(
        kernel,
        out_shape=[jax.ShapeDtypeStruct(new_shape, F32), jax.ShapeDtypeStruct(factor_shape, F32)],
        in_specs=[SMEM] + [VMEM] * (len(chunks) * parts + len(alone)),
        out_specs=[VMEM] * 2,
        compiler_params=params(),
        name="collect_blocks",
    )(me, *[x for c in blocks for x in c], *[factors[c][k] for c, k in alone])


def collect_coeffs(me, coeffs, chunks, shape, parts):
    per_part = shape[1] // parts

    def kernel(me_ref, *refs):
        for c, (g0, groups) in enumerate(chunks):
            for k in range(parts):
                for g in range(groups):
                    for m in range(shape[0]):
                        refs[-1][m, (me_ref[0] ^ k) * per_part + g0 + g] = (
                            refs[c * parts + k][g, :, m * GROUP:(m + 1) * GROUP].T)

    return pl.pallas_call(
        kernel,
        out_shape=jax.ShapeDtypeStruct(shape, F32),
        in_specs=[SMEM] + [VMEM] * (len(chunks) * parts),
        out_specs=VMEM,
        compiler_params=params(),
        name="collect_coeffs",
    )(me, *[x for c in coeffs for x in c])


class Sum:
    def __init__(self, value):
        self.shape = value.shape
        self.value = value.reshape(-1, value.shape[-1])
        self.side = lax.axis_index("blk") % 2
        whole = [k for k in (1 << i for i in range(16)) if k < lax.axis_size("blk")]
        long = self.value.shape[0] > HALVED and len(whole) > 1
        self.steps = ["halve", *whole[1:], "join"] if long else whole

    def step(self):
        kind = self.steps.pop(0)
        if kind == "halve":
            half = self.value.shape[0] // 2
            kept = lax.dynamic_slice_in_dim(self.value, self.side * half, half, 0)
            sent = lax.dynamic_slice_in_dim(self.value, (1 - self.side) * half, half, 0)
            self.value = kept + swap(sent, "blk", 1)
        elif kind == "join":
            other = swap(self.value, "blk", 1)
            first = self.side == 0
            self.value = jnp.concatenate(
                [jnp.where(first, self.value, other), jnp.where(first, other, self.value)], 0)
        else:
            self.value = self.value + swap(self.value, "blk", kind)

    def result(self):
        while self.steps:
            self.step()
        return self.value.reshape(self.shape)


def local(strips, near_cols, vector_block, basis):
    local_blocks = strips.shape[0]
    devices = lax.axis_size("blk")
    parts = lax.axis_size("rhs")
    hops = -(-BAND // local_blocks)
    rows, total = vector_block.shape
    step = total // parts
    groups = step // GROUP
    orders = basis.shape[0]
    chunks = [(0, groups - groups // 2), (groups - groups // 2, groups // 2)]
    chunks = [chunk for chunk in chunks if chunk[1]]
    me = lax.axis_index("rhs").astype(jnp.int32).reshape(1)
    blk = lax.axis_index("blk")
    others = list(range(1, parts))
    relayed = two_lines(devices, hops) and len(chunks) == 2

    table = plan_window(devices, hops)
    place = jnp.asarray(table)[blk][near_cols // local_blocks]
    inside = near_cols % local_blocks
    places = place * local_blocks + inside
    count = int(table.max()) + 1
    early = count - 2
    early_places = jnp.where(place < early, places, early * local_blocks)
    listed = list_late(place, inside, early, count, local_blocks)
    ends = jnp.where((blk < 2) | (blk >= devices - 2), 1, 0).astype(jnp.int32).reshape(1)

    vector = vector_block[None]
    half = -(-orders // 2)
    values = {}

    def send(key):
        kind, at, k = key
        values[key] = swap(values["cut", kind, at, k], "rhs", k)

    def cut(kind, at, value, layer, layers, c0, width):
        for k, x in zip(others, cut_columns(
                value, layer, layers, me, others, c0, width, parts)):
            values["cut", kind, at, k] = x

    def join(kind, at, value, layer, layers, c0, width):
        got = [values[kind, at, k] for k in others]
        return join_rows(value, layer, layers, got, me, c0, width, parts, kind == "b")

    def own_rows(c):
        c0, width = chunks[c][0] * GROUP, chunks[c][1] * GROUP
        values["own", c] = join("v", c, vector, 0, 1, c0, width)[0][0]

    for c, (g0, n) in enumerate(chunks):
        cut("v", c, vector, 0, 1, g0 * GROUP, n * GROUP)
    layers = [(m, min(half, orders - m)) for m in range(0, orders, half)]
    for h, (m, n) in enumerate(layers):
        cut("b", h, basis, m, n, 0, step)

    def barrier(flying=()):
        keys = [key for key in values if key not in flying]
        for key, x in zip(keys, lax.optimization_barrier(tuple(values[k] for k in keys))):
            values[key] = x

    def window(c, names=PLACES):
        return [[values[n, c] for n in alternatives] for alternatives in names]

    for k in others:
        send(("v", 0, k))
    own_rows(0)
    if relayed:
        plan = relay_plan()
        beside = {h: [("b", h, 1)] for h in range(len(layers))}
        for i, (h, k) in enumerate((h, k) for h in range(len(layers)) for k in others if k > 1):
            beside.setdefault(i, []).append(("b", h, k))
        def join_basis(h):
            values["high", h], values["low", h] = join("b", h, basis, *layers[h], 0, step)

        def basis_parts():
            return [(values["high", h], values["low", h]) for h in range(len(layers))]

        def early_part(c):
            values["begun", c] = apply(early_places, ends, strips, window(c, PLACES[:early]))

        def late_part(c):
            return apply_late(
                listed, ends, strips, window(c, PLACES[early:]), values.pop(("begun", c)))

        def early_part(c):
            values["begun", c] = apply(early_places, ends, strips, window(c, PLACES[:early]))

        def late_part(c):
            values["image", c] = apply_late(
                listed, ends, strips, window(c, PLACES[early:]), values.pop(("begun", c)))

        def relay(name, c):
            source, pairs = plan[name]
            if isinstance(source, tuple):
                value = jnp.where(ends[0] == 0, *[values[x, c] for x in source])
            else:
                value = values[source, c]
            values[name, c] = lax.ppermute(value, "blk", pairs)

        def add_step(running):
            running.value = values["sum"]
            running.step()
            values["sum"] = running.value

        for r, relays in enumerate(ROUNDS):
            flying = list(beside.get(r, ()))
            for name, c in relays:
                relay(name, c)
            if r == 0:
                for k in others:
                    send(("v", 1, k))
                own_rows(1)
            for key in flying:
                send(key)
            if r == 3:
                join_basis(0)
            if r == 4:
                for h in range(1, len(layers)):
                    join_basis(h)
                values["image", 0] = apply(places, ends, strips, window(0))
                values["sum"] = inner(values["image", 0], 0, basis_parts(), *chunks[0])
            if r == 5:
                first = Sum(values["sum"])
                first.step()
                values["sum"] = first.value
                early_part(1)
            barrier(flying)
        basis_rows = basis_parts()
    else:
        for c in range(1, len(chunks)):
            for k in others:
                send(("v", c, k))
            own_rows(c)
        for h in range(len(layers)):
            for k in others:
                send(("b", h, k))
        basis_rows = [join("b", h, basis, m, n, 0, step) for h, (m, n) in enumerate(layers)]
        for c in range(len(chunks)):
            pieces = []
            for offset in window_offsets(devices, hops):
                pairs = [((i + offset) % devices, i) for i in range(devices)]
                own = values["own", c]
                pieces.append([lax.ppermute(own, "blk", pairs) if offset else own])
            values["image", c] = apply(places, ends, strips, pieces)

    def spread(value):
        got = [value]
        for k in (1 << i for i in range(16)):
            if 1 < k < parts:
                got += [swap(x, "rhs", k) for x in got]
        pair = [swap(x, "rhs", 1) for x in got]
        return [x for two in zip(got, pair) for x in two]

    def tied(*xs):
        return lax.optimization_barrier(tuple(xs))

    def tie(*running):
        for one, x in zip(running, tied(*[one.value for one in running])):
            one.value = x

    def projected(c, coeffs_t):
        g0, n = chunks[c]
        all_coeffs.append(spread(coeffs_t))
        residual, gram = project(values["image", c], 0, basis_rows, coeffs_t, g0, n)
        residuals.append(residual)
        return Sum(gram)

    all_coeffs, residuals, blocks = [], [], []
    last = len(chunks) - 1
    if relayed:
        first.value = values["sum"]
        first.step()
        late_part(1)
        first.value, values["image", 1] = tied(first.value, values["image", 1])
        first.step()
        second = Sum(inner(values["image", 1], 0, basis_rows, *chunks[1]))
        second.step()
        second.step()
        first.step()
        tie(first, second)
        second.step()
        grams = [projected(0, first.result())]
        tie(second, grams[0])
        second.step()
        grams[0].step()
        tie(second, grams[0])
        grams.append(projected(1, second.result()))
        grams[0].step()
        tie(*grams)
    else:
        grams = [
            projected(c, Sum(inner(values["image", c], 0, basis_rows, *chunks[c])).result())
            for c in range(len(chunks))]
    def finished(c, gram):
        out = list(finish(me, gram, residuals[c], parts))
        if c and relayed:
            for k in others[1:]:
                out[k], blocks[0][k] = tied(out[k], blocks[0][k])
        return [out[0]] + [swap(out[k], "rhs", k) for k in others]

    if relayed:
        blocks.append(finished(0, grams[0].result()))
    held = [x for got in all_coeffs for x in got]
    gram, *held = tied(grams[-1].result(), *held)
    all_coeffs = [held[c * parts:(c + 1) * parts] for c in range(len(chunks))]
    for c in range(len(blocks), len(chunks)):
        blocks.append(finished(c, gram if c == last else grams[c].result()))

    coeffs = collect_coeffs(
        me, all_coeffs, chunks, (orders, total // GROUP, GROUP, GROUP), parts)
    factors = []
    for c, got in enumerate(blocks):
        far = {k: got[k ^ 1][rows:] for k in others if not with_factor(k)}
        if c == last and far:
            k = max(far)
            far[k], coeffs = tied(far[k], coeffs)
        factors.append({k: swap(x, "rhs", 1) for k, x in far.items()})
    new_block, factor = collect_blocks(
        me, blocks, factors, chunks, (rows, total), (total // GROUP, GROUP, GROUP), parts)
    return new_block, coeffs, factor


def solution(mesh):
    placed = (
        P("blk", None, None, None),
        P("blk", None),
        P(("blk", "rhs"), None),
        P(None, ("blk", "rhs"), None),
    )
    return jax.shard_map(
        local,
        mesh=mesh,
        in_specs=placed,
        out_specs=(P(("blk", "rhs"), None), P(), P()),
        check_vma=False,
    )
```

```python
import functools

import jax
import jax.numpy as jnp
import numpy as np
from jax import lax
from jax.experimental import pallas as pl
from jax.experimental.pallas import tpu as pltpu
from jax.sharding import PartitionSpec as P

GROUP = 128
BAND = 24
PANEL = 32
AHEAD = 8
TOGETHER = 8
HALVED = 128

F32 = jnp.float32
BF16 = jnp.bfloat16
ANY = pl.BlockSpec(memory_space=pl.ANY)
SMEM = pl.BlockSpec(memory_space=pltpu.SMEM)
VMEM = pl.BlockSpec(memory_space=pltpu.VMEM)
LIMIT = 50 * 1024 * 1024


def params(**kw):
    return pltpu.CompilerParams(vmem_limit_bytes=LIMIT, **kw)


def pairs_of(axis, k):
    return [(i, i ^ k) for i in range(lax.axis_size(axis))]


def swap(value, axis, k):
    return lax.ppermute(value, axis, pairs_of(axis, k))


def split(value):
    high = value.astype(BF16)
    return high, (value - high.astype(F32)).astype(BF16)


def dot3(a, b, dims):
    return dot3_parts(split(a), split(b), dims)


def dot3_parts(a, b, dims):
    (a_high, a_low), (b_high, b_low) = a, b

    def one(x, y):
        return lax.dot_general(x, y, (dims, ((), ())), preferred_element_type=F32)

    return one(a_high, b_high) + (one(a_high, b_low) + one(a_low, b_high))


def aligned(index, step):
    return pl.ds(pl.multiple_of(index * step, step), step)


def column_spec(value, layer, parts, k):
    rows, step = value.shape[1], value.shape[2] // parts
    return pl.BlockSpec((1, rows, step), lambda i, me: (layer + i, 0, me[0] ^ k))


def layer_spec(rows, width):
    return pl.BlockSpec((1, rows, width), lambda i, me: (i, 0, 0))


def cut_columns(value, layer, layers, me, ks, c0, width, parts, after=()):
    rows = value.shape[1]

    def kernel(me_ref, *refs):
        for src, dst in zip(refs, refs[-len(ks):]):
            dst[...] = src[:, :, c0:c0 + width]

    return pl.pallas_call(
        kernel,
        grid_spec=pltpu.PrefetchScalarGridSpec(
            num_scalar_prefetch=1,
            grid=(layers,),
            in_specs=[column_spec(value, layer, parts, k) for k in ks] + [ANY] * len(after),
            out_specs=[layer_spec(rows, width)] * len(ks),
        ),
        out_shape=[jax.ShapeDtypeStruct((layers, rows, width), value.dtype)] * len(ks),
        compiler_params=params(),
        name="cut_columns",
    )(me, *[value] * len(ks), *after)


def join_rows(value, layer, layers, received, me, c0, width, parts, halves=False):
    rows = value.shape[1]
    types = [BF16, BF16] if halves else [value.dtype]

    def kernel(me_ref, *refs):
        for k in range(parts):
            at = c0 if k == 0 else 0
            piece = refs[k][0, :, at:at + width]
            for out, x in zip(refs[parts:], split(piece) if halves else [piece]):
                out[0, aligned(me_ref[0] ^ k, rows), :] = x

    return pl.pallas_call(
        kernel,
        grid_spec=pltpu.PrefetchScalarGridSpec(
            num_scalar_prefetch=1,
            grid=(layers,),
            in_specs=[column_spec(value, layer, parts, 0)]
            + [layer_spec(rows, width)] * (parts - 1),
            out_specs=[layer_spec(rows * parts, width)] * len(types),
        ),
        out_shape=[jax.ShapeDtypeStruct((layers, rows * parts, width), t) for t in types],
        compiler_params=params(),
        name="join_rows",
    )(me, value, *received)


def two_lines(devices, hops):
    return devices == 8 and devices == 2 * hops + 2


def window_offsets(devices, hops):
    seen = []
    for offset in range(-hops, hops + 1):
        if offset % devices not in seen:
            seen.append(offset % devices)
    return sorted(seen, key=lambda offset: min(offset, devices - offset))


def plan_window(devices, hops):
    table = np.zeros((devices, devices), np.int32)
    if two_lines(devices, hops):
        for z in range(4):
            for y in range(2):
                inner, far, back = z in (1, 2), 3 - z, 1 - y
                places = [
                    (z, y), (z ^ 1, y), (z, back), (z ^ 1, back), (far, back if inner else y),
                    (far, y) if inner else (2 if z == 0 else 1, back),
                    (3 if z == 1 else 0, back) if inner else (far, back),
                ]
                for place, (a, b) in enumerate(places):
                    table[2 * z + y, 2 * a + b] = place
        return table
    for d in range(devices):
        for place, offset in enumerate(window_offsets(devices, hops)):
            table[d, (d + offset) % devices] = place
    return table


def relay_plan():
    def lines(pairs):
        return [(2 * a + y, 2 * b + y) for a, b in pairs for y in (0, 1)]

    outer = lines([(0, 1), (1, 0), (2, 3), (3, 2)])
    middle = lines([(1, 2), (2, 1)])
    to_ends = lines([(1, 0), (2, 3)])
    across = [(i, i ^ 1) for i in range(8)]
    return {
        "q1": ("own", outer), "y1": ("own", across), "q2": ("own", middle),
        "q3": ("q1", middle), "y2": ("q1", across), "q5": ("y1", middle),
        "q4": ("q3", to_ends), "q6": ("q5", to_ends),
        "y3": (("q3", "q4"), across),
    }


ROUNDS = (
    (("y1", 0), ("q1", 0), ("q2", 0)),
    (("q1", 1), ("y2", 0), ("q3", 0)),
    (("q4", 0), ("y1", 1), ("q5", 0)),
    (("q6", 0), ("q3", 1), ("y3", 0)),
    (("q4", 1), ("y2", 1), ("q5", 1)),
    (("q6", 1), ("q2", 1), ("y3", 1)),
)
PLACES = (("own",), ("q1",), ("y1",), ("y2",), ("q5", "q4"), ("q2", "q6"), ("y3",))


def load_window(pieces, counts, ends, raw, window, sems, block):
    rows = raw.shape[1]
    at = 0
    for place, count in enumerate(counts):
        for end in range(count):
            def fetch(at=at, place=place, end=end):
                pltpu.make_async_copy(pieces[at + end], raw.at[place], sems.at[place]).start()

            if count == 1:
                fetch()
            else:
                pl.when(ends[0] == end)(fetch)
        at += count
    for place in range(len(counts)):
        pltpu.make_async_copy(pieces[0], raw.at[place], sems.at[place]).wait()

        def one(i, carry, place=place):
            high, low = split(raw[place, aligned(i, block), :])
            base = (place * (rows // block) + i) * 2
            window[aligned(base, block), :] = high
            window[aligned(base + 1, block), :] = low
            return carry

        lax.fori_loop(0, rows // block, one, 0)


def four_terms(strip):
    high, low = split(strip)
    return jnp.concatenate(
        [jnp.concatenate([high, high], 1), jnp.concatenate([low, low], 1)], 0)


def apply_kernel(counts, near, places, ends, strips, *rest):
    pieces = rest[:sum(counts)]
    image, raw, window, sems = rest[sum(counts):]
    step = pl.program_id(0)
    block = strips.shape[2]

    @pl.when(step == 0)
    def _():
        load_window(pieces, counts, ends, raw, window, sems, block)
        window[len(counts) * raw.shape[1] * 2:, :] = jnp.zeros((2 * block, raw.shape[2]), BF16)

    total = jnp.zeros((2 * block, raw.shape[2]), F32)
    for k in range(near):
        right = window[aligned(places[step, k], 2 * block), :]
        total = total + jnp.dot(four_terms(strips[0, k]), right, preferred_element_type=F32)
    image[...] = total[:block] + total[block:]


def group_specs(basis_rows, tile, g0, groups):
    specs, arrays = [], []
    for g in range(g0, g0 + groups):
        for part in (0, 1):
            for two in basis_rows:
                for m in range(two[part].shape[0]):
                    specs.append(pl.BlockSpec((1, tile, GROUP), lambda i, m=m, g=g: (m, i, g)))
                    arrays.append(two[part])
    return specs, arrays


def wide_parts(basis, orders, g):
    at = 2 * orders * g
    return [
        jnp.concatenate([x[0] for x in basis[at + p * orders:at + (p + 1) * orders]], 1)
        for p in (0, 1)]


def apply(places, ends, strips, pieces):
    row_blocks, near, block, _ = strips.shape
    rows, width = pieces[0][0].shape
    counts = [len(p) for p in pieces]
    flat = [x for p in pieces for x in p]
    return pl.pallas_call(
        functools.partial(apply_kernel, counts, near),
        grid=(row_blocks,),
        out_shape=jax.ShapeDtypeStruct((rows, width), F32),
        in_specs=[SMEM, SMEM, pl.BlockSpec((1, near, block, block), lambda i: (i, 0, 0, 0))]
        + [ANY] * len(flat),
        out_specs=pl.BlockSpec((block, width), lambda i: (i, 0)),
        scratch_shapes=[
            pltpu.VMEM((len(counts), rows, width), F32),
            pltpu.VMEM((len(counts) * rows * 2 + 2 * block, width), BF16),
            pltpu.SemaphoreType.DMA((len(counts),)),
        ],
        compiler_params=params(),
        cost_estimate=pl.CostEstimate(
            flops=8 * row_blocks * near * block * block * width,
            bytes_accessed=strips.size * 4 + 8 * rows * width * 4, transcendentals=0),
        name="apply",
    )(places, ends, strips, *flat)


def apply_late_kernel(counts, chosen, found, number, ends, begun, strips, *rest):
    pieces = rest[:sum(counts)]
    image, raw, window, held, total, before, sems, strip_sems = rest[sum(counts):]
    row_blocks, room, block, _ = held.shape
    rows, width = raw.shape[1], raw.shape[2]

    def copy(i, j):
        return pltpu.make_async_copy(strips.at[i, chosen[i, j]], held.at[i, j], strip_sems.at[i, j])

    def each(i, do):
        for j0 in range(0, room, TOGETHER):
            @pl.when(j0 < number[i])
            def _(j0=j0):
                do(range(j0, j0 + TOGETHER))

    def start(i, carry):
        def do(js):
            for j in js:
                copy(i, j).start()

        each(i, do)
        return carry

    bring = pltpu.make_async_copy(begun, before, sems.at[len(counts)])
    bring.start()
    lax.fori_loop(0, row_blocks, start, 0)
    load_window(pieces, counts, ends, raw, window, sems, block)
    window[len(counts) * rows * 2:, :] = jnp.zeros((2 * block, width), BF16)

    bring.wait()

    def one(i, carry):
        total[:block] = before[aligned(i, block), :]
        total[block:] = jnp.zeros((block, width), F32)

        def do(js):
            for j in js:
                copy(i, j).wait()
            left = jnp.concatenate([four_terms(held[i, j]) for j in js], 1)
            right = jnp.concatenate(
                [window[aligned(found[i, j], 2 * block), :] for j in js], 0)
            total[...] += jnp.dot(left, right, preferred_element_type=F32)

        each(i, do)
        image[aligned(i, block), :] = total[:block] + total[block:]
        return carry

    lax.fori_loop(0, row_blocks, one, 0)


def apply_late(listed, ends, strips, pieces, begun):
    row_blocks, _, block, _ = strips.shape
    rows, width = begun.shape
    room = listed[0].shape[1]
    counts = [len(p) for p in pieces]
    flat = [x for p in pieces for x in p]
    return pl.pallas_call(
        functools.partial(apply_late_kernel, counts),
        out_shape=jax.ShapeDtypeStruct((rows, width), F32),
        in_specs=[SMEM] * 4 + [ANY] * (2 + len(flat)),
        out_specs=VMEM,
        scratch_shapes=[
            pltpu.VMEM((len(counts), rows, width), F32),
            pltpu.VMEM((len(counts) * rows * 2 + 2 * block, width), BF16),
            pltpu.VMEM((row_blocks, room, block, block), F32),
            pltpu.VMEM((2 * block, width), F32),
            pltpu.VMEM((rows, width), F32),
            pltpu.SemaphoreType.DMA((len(counts) + 1,)),
            pltpu.SemaphoreType.DMA((row_blocks, room)),
        ],
        compiler_params=params(),
        cost_estimate=pl.CostEstimate(
            flops=4 * row_blocks * room * block * block * width,
            bytes_accessed=8 * rows * width * 4, transcendentals=0),
        name="apply_late",
    )(*listed, ends, begun, strips, *flat)


def list_late(place, inside, early, count, local_blocks):
    near = place.shape[1]
    most = min(near, (count - early) * local_blocks)
    room = -(-most // TOGETHER) * TOGETHER
    late = place >= early
    number = jnp.sum(late, axis=1, dtype=jnp.int32)
    rank = jnp.cumsum(late, axis=1, dtype=jnp.int32) - 1
    slots = jnp.arange(room)
    picked = (late & (slots[:, None, None] == rank)).astype(jnp.int32)
    chosen = jnp.sum(picked * jnp.arange(near), axis=2, dtype=jnp.int32).T
    found = jnp.sum(picked * ((place - early) * local_blocks + inside), axis=2, dtype=jnp.int32).T
    found = jnp.where(slots < number[:, None], found, (count - early) * local_blocks)
    return chosen, found, number


def inner_kernel(orders, image, *rest):
    basis, partial = rest[:-1], rest[-1]

    @pl.when(pl.program_id(0) == 0)
    def _():
        partial[...] = jnp.zeros_like(partial)

    for g in range(partial.shape[0]):
        cols = slice(g * GROUP, (g + 1) * GROUP)
        partial[g] += dot3_parts(
            split(image[:, cols]), wide_parts(basis, orders, g), ((0,), (0,)))


def inner(image, at, basis_rows, g0, groups):
    rows, width = image.shape[0], groups * GROUP
    orders = sum(two[0].shape[0] for two in basis_rows)
    tile = rows // 2
    specs, arrays = group_specs(basis_rows, tile, g0, groups)
    shape = (groups, GROUP, orders * GROUP)
    return pl.pallas_call(
        functools.partial(inner_kernel, orders),
        grid=(rows // tile,),
        out_shape=jax.ShapeDtypeStruct(shape, F32),
        in_specs=[pl.BlockSpec((tile, width), lambda i: (i, at // groups))] + specs,
        out_specs=pl.BlockSpec(shape, lambda i: (0, 0, 0)),
        compiler_params=params(),
        cost_estimate=pl.CostEstimate(
            flops=24 * rows * width * GROUP, bytes_accessed=5 * rows * width * 4,
            transcendentals=0),
        name="inner",
    )(image, *arrays)


def project_kernel(orders, image, coeffs_t, *rest):
    groups = coeffs_t.shape[0]
    basis, (residual, gram) = rest[:-2], rest[-2:]

    @pl.when(pl.program_id(0) == 0)
    def _():
        gram[...] = jnp.zeros_like(gram)

    for g in range(groups):
        cols = slice(g * GROUP, (g + 1) * GROUP)
        left = image[:, cols] - dot3_parts(
            wide_parts(basis, orders, g), split(coeffs_t[g]), ((1,), (1,)))
        residual[:, cols] = left
        parts = split(left)
        gram[g] += dot3_parts(parts, parts, ((0,), (0,)))


def project(image, at, basis_rows, coeffs_t, g0, groups):
    orders = sum(two[0].shape[0] for two in basis_rows)
    rows, width = image.shape[0], groups * GROUP
    tile = rows // 2
    specs, arrays = group_specs(basis_rows, tile, g0, groups)
    return pl.pallas_call(
        functools.partial(project_kernel, orders),
        grid=(rows // tile,),
        out_shape=[
            jax.ShapeDtypeStruct((rows, width), F32),
            jax.ShapeDtypeStruct((groups, GROUP, GROUP), F32),
        ],
        in_specs=[
            pl.BlockSpec((tile, width), lambda i: (i, at // groups)),
            pl.BlockSpec(coeffs_t.shape, lambda i: (0, 0, 0)),
        ] + specs,
        out_specs=[
            pl.BlockSpec((tile, width), lambda i: (i, 0)),
            pl.BlockSpec((groups, GROUP, GROUP), lambda i: (0, 0, 0)),
        ],
        compiler_params=params(),
        cost_estimate=pl.CostEstimate(
            flops=30 * rows * width * GROUP, bytes_accessed=6 * rows * width * 4,
            transcendentals=0),
        name="project",
    )(image, coeffs_t, *arrays)


def eliminate(gram):
    count = len(gram)
    order = gram[0].shape[0]
    row_at = lax.broadcasted_iota(jnp.int32, (order, order), 0)
    col_at = lax.broadcasted_iota(jnp.int32, (order, order), 1)
    eye = jnp.where(row_at == col_at, 1.0, 0.0).astype(F32)
    rest = [jnp.concatenate([g, eye], 1) for g in gram]
    done = [[] for _ in gram]
    panel_row = lax.broadcasted_iota(jnp.int32, (PANEL, order), 0)
    for p0 in range(0, order, PANEL):
        panels = [r[:PANEL] for r in rest]
        inverse_pivots = [[] for _ in gram]
        for j0 in range(0, PANEL, AHEAD):
            ahead = [
                [jnp.broadcast_to(panel[:, p0 + j:p0 + j + 1], (PANEL, order))
                 for j in range(j0, j0 + AHEAD)] for panel in panels]
            for t in range(AHEAD):
                j = j0 + t
                for n in range(count):
                    columns, panel = ahead[n], panels[n]
                    inverse = 1.0 / columns[t][j:j + 1]
                    factor = jnp.where(panel_row > j, columns[t] * inverse, 0.0)
                    for u in range(t + 1, AHEAD):
                        columns[u] = columns[u] - factor * columns[u][j:j + 1]
                    panels[n] = panel - jnp.concatenate([factor, factor], 1) * panel[j:j + 1]
                    inverse_pivots[n].append(inverse)
        for n in range(count):
            scale = jnp.sqrt(jnp.concatenate(inverse_pivots[n], 0))
            panel = panels[n] * jnp.concatenate([scale, scale], 1)
            done[n].append(panel)
            if p0 + PANEL < order:
                below = panel[:, p0 + PANEL:order]
                rest[n] = rest[n][PANEL:] - lax.dot_general(
                    below, panel, (((0,), (0,)), ((), ())),
                    precision=lax.Precision.HIGHEST, preferred_element_type=F32)
    lowers, inverses = [], []
    for n in range(count):
        upper = jnp.concatenate(done[n], 0)
        lowers.append(jnp.where(row_at >= col_at, upper[:, :order].T, 0.0))
        inverses.append(upper[:, order:])
    return lowers, inverses


def with_factor(k):
    return k < 2 or not k & 1


def finish_kernel(groups, parts, me, gram, residual, *outs):
    lowers, inverses = eliminate([gram[g] for g in range(groups)])
    rows = residual.shape[0] // parts
    for k in range(parts):
        for g in range(groups):
            cols = slice(g * GROUP, (g + 1) * GROUP)
            left = residual[aligned(me[0] ^ k, rows), cols]
            outs[k][:rows, cols] = dot3(left, inverses[g], ((1,), (1,)))
            if with_factor(k):
                outs[k][rows:, cols] = lowers[g]


def finish(me, gram, residual, parts):
    groups = gram.shape[0]
    rows, width = residual.shape
    shapes = [
        jax.ShapeDtypeStruct((rows // parts + GROUP * with_factor(k), width), F32)
        for k in range(parts)]
    return pl.pallas_call(
        functools.partial(finish_kernel, groups, parts),
        out_shape=shapes,
        in_specs=[SMEM, VMEM, VMEM],
        out_specs=[VMEM] * parts,
        compiler_params=params(),
        cost_estimate=pl.CostEstimate(
            flops=6 * rows * width * GROUP, bytes_accessed=4 * rows * width * 4,
            transcendentals=0),
        name="finish",
    )(me, gram, residual)


def collect_blocks(me, blocks, factors, chunks, new_shape, factor_shape, parts):
    rows = new_shape[0]
    step = new_shape[1] // parts
    per_part = step // GROUP
    alone = [(c, k) for c in range(len(chunks)) for k in range(parts) if not with_factor(k)]

    def kernel(me_ref, *refs):
        new_out, factor_out = refs[-2:]
        for c, (g0, groups) in enumerate(chunks):
            for k in range(parts):
                src = refs[c * parts + k]
                at = me_ref[0] ^ k
                if (c, k) in alone:
                    factor = refs[len(chunks) * parts + alone.index((c, k))]
                else:
                    factor = src.at[pl.ds(rows, GROUP), :]
                for g in range(groups):
                    cols = slice(g * GROUP, (g + 1) * GROUP)
                    group = at * per_part + g0 + g
                    new_out[:, aligned(group, GROUP)] = src[:rows, cols]
                    factor_out[group] = factor[:, cols]

    return pl.pallas_call(
        kernel,
        out_shape=[jax.ShapeDtypeStruct(new_shape, F32), jax.ShapeDtypeStruct(factor_shape, F32)],
        in_specs=[SMEM] + [VMEM] * (len(chunks) * parts + len(alone)),
        out_specs=[VMEM] * 2,
        compiler_params=params(),
        name="collect_blocks",
    )(me, *[x for c in blocks for x in c], *[factors[c][k] for c, k in alone])


def collect_coeffs(me, coeffs, chunks, shape, parts):
    per_part = shape[1] // parts

    def kernel(me_ref, *refs):
        for c, (g0, groups) in enumerate(chunks):
            for k in range(parts):
                for g in range(groups):
                    for m in range(shape[0]):
                        refs[-1][m, (me_ref[0] ^ k) * per_part + g0 + g] = (
                            refs[c * parts + k][g, :, m * GROUP:(m + 1) * GROUP].T)

    return pl.pallas_call(
        kernel,
        out_shape=jax.ShapeDtypeStruct(shape, F32),
        in_specs=[SMEM] + [VMEM] * (len(chunks) * parts),
        out_specs=VMEM,
        compiler_params=params(),
        name="collect_coeffs",
    )(me, *[x for c in coeffs for x in c])


class Sum:
    def __init__(self, value):
        self.shape = value.shape
        self.value = value.reshape(-1, value.shape[-1])
        self.side = lax.axis_index("blk") % 2
        whole = [k for k in (1 << i for i in range(16)) if k < lax.axis_size("blk")]
        long = self.value.shape[0] > HALVED and len(whole) > 1
        self.steps = ["halve", *whole[1:], "join"] if long else whole

    def step(self):
        kind = self.steps.pop(0)
        if kind == "halve":
            half = self.value.shape[0] // 2
            kept = lax.dynamic_slice_in_dim(self.value, self.side * half, half, 0)
            sent = lax.dynamic_slice_in_dim(self.value, (1 - self.side) * half, half, 0)
            self.value = kept + swap(sent, "blk", 1)
        elif kind == "join":
            other = swap(self.value, "blk", 1)
            first = self.side == 0
            self.value = jnp.concatenate(
                [jnp.where(first, self.value, other), jnp.where(first, other, self.value)], 0)
        else:
            self.value = self.value + swap(self.value, "blk", kind)

    def result(self):
        while self.steps:
            self.step()
        return self.value.reshape(self.shape)


def local(strips, near_cols, vector_block, basis):
    local_blocks = strips.shape[0]
    devices = lax.axis_size("blk")
    parts = lax.axis_size("rhs")
    hops = -(-BAND // local_blocks)
    rows, total = vector_block.shape
    step = total // parts
    groups = step // GROUP
    orders = basis.shape[0]
    chunks = [(0, groups - groups // 2), (groups - groups // 2, groups // 2)]
    chunks = [chunk for chunk in chunks if chunk[1]]
    me = lax.axis_index("rhs").astype(jnp.int32).reshape(1)
    blk = lax.axis_index("blk")
    others = list(range(1, parts))
    relayed = two_lines(devices, hops) and len(chunks) == 2

    table = plan_window(devices, hops)
    place = jnp.asarray(table)[blk][near_cols // local_blocks]
    inside = near_cols % local_blocks
    places = place * local_blocks + inside
    count = int(table.max()) + 1
    early = count - 2
    early_places = jnp.where(place < early, places, early * local_blocks)
    listed = list_late(place, inside, early, count, local_blocks)
    ends = jnp.where((blk < 2) | (blk >= devices - 2), 1, 0).astype(jnp.int32).reshape(1)

    vector = vector_block[None]
    half = -(-orders // 2)
    values = {}

    def send(key):
        kind, at, k = key
        values[key] = swap(values["cut", kind, at, k], "rhs", k)

    def cut(kind, at, value, layer, layers, c0, width):
        for k, x in zip(others, cut_columns(
                value, layer, layers, me, others, c0, width, parts)):
            values["cut", kind, at, k] = x

    def join(kind, at, value, layer, layers, c0, width):
        got = [values[kind, at, k] for k in others]
        return join_rows(value, layer, layers, got, me, c0, width, parts, kind == "b")

    def own_rows(c):
        c0, width = chunks[c][0] * GROUP, chunks[c][1] * GROUP
        values["own", c] = join("v", c, vector, 0, 1, c0, width)[0][0]

    for c, (g0, n) in enumerate(chunks):
        cut("v", c, vector, 0, 1, g0 * GROUP, n * GROUP)
    layers = [(m, min(half, orders - m)) for m in range(0, orders, half)]
    for h, (m, n) in enumerate(layers):
        cut("b", h, basis, m, n, 0, step)

    def barrier(flying=()):
        keys = [key for key in values if key not in flying]
        for key, x in zip(keys, lax.optimization_barrier(tuple(values[k] for k in keys))):
            values[key] = x

    def window(c, names=PLACES):
        return [[values[n, c] for n in alternatives] for alternatives in names]

    for k in others:
        send(("v", 0, k))
    own_rows(0)
    if relayed:
        plan = relay_plan()
        beside = {h: [("b", h, 1)] for h in range(len(layers))}
        for i, (h, k) in enumerate((h, k) for h in range(len(layers)) for k in others if k > 1):
            beside.setdefault(i, []).append(("b", h, k))
        def join_basis(h):
            values["high", h], values["low", h] = join("b", h, basis, *layers[h], 0, step)

        def basis_parts():
            return [(values["high", h], values["low", h]) for h in range(len(layers))]

        def early_part(c):
            values["begun", c] = apply(early_places, ends, strips, window(c, PLACES[:early]))

        def late_part(c):
            return apply_late(
                listed, ends, strips, window(c, PLACES[early:]), values.pop(("begun", c)))

        def early_part(c):
            values["begun", c] = apply(early_places, ends, strips, window(c, PLACES[:early]))

        def late_part(c):
            values["image", c] = apply_late(
                listed, ends, strips, window(c, PLACES[early:]), values.pop(("begun", c)))

        def relay(name, c):
            source, pairs = plan[name]
            if isinstance(source, tuple):
                value = jnp.where(ends[0] == 0, *[values[x, c] for x in source])
            else:
                value = values[source, c]
            values[name, c] = lax.ppermute(value, "blk", pairs)

        def add_step(running):
            running.value = values["sum"]
            running.step()
            values["sum"] = running.value

        for r, relays in enumerate(ROUNDS):
            flying = list(beside.get(r, ()))
            for name, c in relays:
                relay(name, c)
            if r == 0:
                for k in others:
                    send(("v", 1, k))
                own_rows(1)
            for key in flying:
                send(key)
            if r == 3:
                join_basis(0)
            if r == 4:
                for h in range(1, len(layers)):
                    join_basis(h)
                values["image", 0] = apply(places, ends, strips, window(0))
                values["sum"] = inner(values["image", 0], 0, basis_parts(), *chunks[0])
            if r == 5:
                first = Sum(values["sum"])
                first.step()
                values["sum"] = first.value
                early_part(1)
            barrier(flying)
        basis_rows = basis_parts()
    else:
        for c in range(1, len(chunks)):
            for k in others:
                send(("v", c, k))
            own_rows(c)
        for h in range(len(layers)):
            for k in others:
                send(("b", h, k))
        basis_rows = [join("b", h, basis, m, n, 0, step) for h, (m, n) in enumerate(layers)]
        for c in range(len(chunks)):
            pieces = []
            for offset in window_offsets(devices, hops):
                pairs = [((i + offset) % devices, i) for i in range(devices)]
                own = values["own", c]
                pieces.append([lax.ppermute(own, "blk", pairs) if offset else own])
            values["image", c] = apply(places, ends, strips, pieces)

    def spread(value):
        got = [value]
        for k in (1 << i for i in range(16)):
            if 1 < k < parts:
                got += [swap(x, "rhs", k) for x in got]
        pair = [swap(x, "rhs", 1) for x in got]
        return [x for two in zip(got, pair) for x in two]

    def tied(*xs):
        return lax.optimization_barrier(tuple(xs))

    def tie(*running):
        for one, x in zip(running, tied(*[one.value for one in running])):
            one.value = x

    def projected(c, coeffs_t):
        g0, n = chunks[c]
        all_coeffs.append(spread(coeffs_t))
        residual, gram = project(values["image", c], 0, basis_rows, coeffs_t, g0, n)
        residuals.append(residual)
        return Sum(gram)

    all_coeffs, residuals, blocks = [], [], []
    last = len(chunks) - 1
    if relayed:
        first.value = values["sum"]
        first.step()
        late_part(1)
        first.value, values["image", 1] = tied(first.value, values["image", 1])
        first.step()
        second = Sum(inner(values["image", 1], 0, basis_rows, *chunks[1]))
        second.step()
        second.step()
        first.step()
        tie(first, second)
        second.step()
        grams = [projected(0, first.result())]
        tie(second, grams[0])
        second.step()
        grams[0].step()
        tie(second, grams[0])
        grams.append(projected(1, second.result()))
        grams[0].step()
        tie(*grams)
    else:
        grams = [
            projected(c, Sum(inner(values["image", c], 0, basis_rows, *chunks[c])).result())
            for c in range(len(chunks))]
    def finished(c, gram):
        out = list(finish(me, gram, residuals[c], parts))
        if c and relayed:
            for k in others[1:]:
                out[k], blocks[0][k] = tied(out[k], blocks[0][k])
        return [out[0]] + [swap(out[k], "rhs", k) for k in others]

    if relayed:
        blocks.append(finished(0, grams[0].result()))
    held = [x for got in all_coeffs for x in got]
    gram, *held = tied(grams[-1].result(), *held)
    all_coeffs = [held[c * parts:(c + 1) * parts] for c in range(len(chunks))]
    for c in range(len(blocks), len(chunks)):
        blocks.append(finished(c, gram if c == last else grams[c].result()))

    coeffs = collect_coeffs(
        me, all_coeffs, chunks, (orders, total // GROUP, GROUP, GROUP), parts)
    factors = []
    for c, got in enumerate(blocks):
        far = {k: got[k ^ 1][rows:] for k in others if not with_factor(k)}
        if c == last and far:
            k = max(far)
            far[k], coeffs = tied(far[k], coeffs)
        factors.append({k: swap(x, "rhs", 1) for k, x in far.items()})
    new_block, factor = collect_blocks(
        me, blocks, factors, chunks, (rows, total), (total // GROUP, GROUP, GROUP), parts)
    return new_block, coeffs, factor


def solution(mesh):
    placed = (
        P("blk", None, None, None),
        P("blk", None),
        P(("blk", "rhs"), None),
        P(None, ("blk", "rhs"), None),
    )
    return jax.shard_map(
        local,
        mesh=mesh,
        in_specs=placed,
        out_specs=(P(("blk", "rhs"), None), P(), P()),
        check_vma=False,
    )
```
